512 devices in a mesh: member: 16 (over x, z_lo), gx: 32 (over y, z_hi, core).
Axes of the slice: x: 4, y: 8, z: 8 (z_hi: 2, z_lo: 4; z = z_hi * 4 + z_lo), core: 2. Of those that a mesh axis runs over, the one named last changes fastest.
Arguments:
- background_fields: float32 [64, 16, 512, 128], P('member', None, 'gx'), may hold values from -6 to 6
- obs_col: int32 [2048], replicated, may hold values from 0 to 65535, as said below
- measured_height: int32 [2048], P('gx'), may hold values from 0 to 3
- obs_radius: int32 [2048], replicated, may hold values from 8 to 16
- obs_value: float32 [2048], P('gx'), may hold values from -8 to 8
- obs_var: float32 [2048], P('gx'), may hold values from 0.005 to 0.05
Outputs:
- analysis: float32 [64, 16, 512, 128], P('member', None, 'gx')
The draws below stay inside these ranges and needn't reach their ends.
Inputs may be any that keep to these rules, and one draw needn't show every extreme that they name: `obs_col`: entries j * 64 to (j + 1) * 64 - 1 observe columns x * 128 + y with x from j * 16 to (j + 1) * 16 - 1.
All inputs are finite; a program needn't handle non-finite values.
Results may differ from the reference program's by a relative error of at most 0.0003.
Values sent between devices are 32-bit elements; how exact they have to be, the bound alone decides.
A program may use at most 64 MiB of HBM per device.

```python
import math
import jax
import jax.numpy as jnp
from jax import lax

LEV = 4
PATCH_CELLS_EAST = 16
NY = 128
NOBS = 64
NS_ITERS = 6
FSTEPS = 2
MEMBERS = 64
FIELDS = 16
NX = 512
NOBS_ALL = 2048
N_GX = 32


def draw_obs_col(key, part):
    key = jax.random.fold_in(key, 11)
    first_key, second_key, third_key, fourth_key = jax.random.split(key, 4)
    tile_of = jnp.arange(NOBS_ALL, dtype=jnp.int32) // NOBS
    local_rows = jax.random.randint(first_key, (NOBS_ALL,), 0, PATCH_CELLS_EAST, dtype=jnp.int32)
    across_cols = jax.random.randint(second_key, (NOBS_ALL,), 0, NY, dtype=jnp.int32)
    cell_stack_group = (tile_of * PATCH_CELLS_EAST + local_rows) * NY + across_cols
    lowest_slot = jax.random.randint(third_key, (), 0, NOBS, dtype=jnp.int32)
    highest_slot = jax.random.randint(fourth_key, (), 0, NOBS, dtype=jnp.int32) + NOBS_ALL - NOBS
    cell_stack_group = cell_stack_group.at[lowest_slot].set(0)
    cell_stack_group = cell_stack_group.at[highest_slot].set(NX * NY - 1)
    return cell_stack_group


def draw_obs_radius(key, part):
    key = jax.random.fold_in(key, 23)
    first_key, second_key, third_key = jax.random.split(key, 3)
    radius_cols = jax.random.randint(first_key, (NOBS_ALL,), PATCH_CELLS_EAST // 2, PATCH_CELLS_EAST + 1, dtype=jnp.int32)
    tile_total = NOBS_ALL // NOBS
    widest = jnp.arange(tile_total, dtype=jnp.int32) * NOBS + jax.random.randint(second_key, (tile_total,), 0, NOBS, dtype=jnp.int32)
    radius_cols = radius_cols.at[widest].set(PATCH_CELLS_EAST)
    narrowest = jax.random.randint(third_key, (), 0, NOBS_ALL, dtype=jnp.int32)
    return radius_cols.at[narrowest].set(PATCH_CELLS_EAST // 2)


def with_ends(values, rng, low, top_value):
    longest = values.shape.index(max(values.shape))
    spots = []
    for shift in (0, 1):
        where = [jax.random.randint(jax.random.fold_in(rng, axis), (), 0, length) for axis, length in enumerate(values.shape)]
        where[longest] = (where[longest] + shift) % values.shape[longest]
        spots.append(tuple(where))
    return values.at[spots[0]].set(low).at[spots[1]].set(top_value)


def levels(stream_key, dims, cuts, smallest, top_value):
    def one(dim, shards_of):
        steps = jax.random.uniform(jax.random.fold_in(jax.random.fold_in(stream_key, 6), dim), (shards_of,), jnp.float32, smallest / len(cuts), top_value / len(cuts))
        return jnp.repeat(jnp.exp(steps), dims[dim] // shards_of).reshape((-1,) + (1,) * (len(dims) - dim - 1))

    loudness = one(*cuts[0])
    for cut in cuts[1:]:
        loudness = loudness * one(*cut)
    return loudness


def scatter_about(rng, extent, scale, limit, shards=(), held_as=jnp.bfloat16):
    factor_of = levels(rng, extent, shards, -0.22, 0.18) if shards else 1.0
    entries = jax.random.normal(rng, extent, jnp.float32) * scale * factor_of
    return jnp.minimum(jnp.maximum(entries, -limit), limit).astype(held_as)


def setup_inputs(seed: int = 0) -> dict:
    seeds = jax.random.split(jax.random.key(seed), 7)
    return {
        "background_fields": scatter_about(seeds[0], (MEMBERS, FIELDS, NX, NY), 1.0, 6.0, ((0, 16), (2, 32)), jnp.float32),
        "obs_col": draw_obs_col(jax.random.fold_in(seeds[6], 71), 0),
        "measured_height": with_ends(jax.random.randint(seeds[2], (NOBS_ALL,), 0, LEV), jax.random.fold_in(seeds[2], 1), 0, LEV - 1).astype(jnp.int32),
        "obs_radius": draw_obs_radius(jax.random.fold_in(seeds[6], 71), 0),
        "obs_value": scatter_about(seeds[4], (NOBS_ALL,), 1.5, 8.0, ((0, 32),), jnp.float32),
        "obs_var": jnp.clip(jnp.exp(math.log(0.05) - 2.3025851 * jax.random.uniform(seeds[5], (NOBS_ALL,), jnp.float32) ** levels(seeds[5], (NOBS_ALL,), ((0, 32),), -0.2, 0.2)), 0.005, 0.05),
    }


COURANT = 0.6
DIFFUSE = 0.1
PRECISE = lax.Precision.HIGHEST

def advance_grid(member_state):
    bordered_fields = jnp.pad(member_state, ((0, 0), (1, 1), (1, 1)))
    center = member_state
    western = bordered_fields[:, :-2, 1:-1]
    eastern = bordered_fields[:, 2:, 1:-1]
    southern = bordered_fields[:, 1:-1, :-2]
    northern = bordered_fields[:, 1:-1, 2:]
    return center + COURANT * (western - center) + DIFFUSE * (western + eastern + southern + northern - 4.0 * center)

def analysis_weights(spread, innovation, inverse, measured_easting, measured_northing, obs_reach, site_along, site_across):
    members = spread.shape[0]
    obs_total = spread.shape[1]
    gap_along = (site_along[:, None] - measured_easting[None, :]).astype(jnp.float32)
    gap_across = (site_across[:, None] - measured_northing[None, :]).astype(jnp.float32)
    radius_cols = obs_reach.astype(jnp.float32)
    taper_weights = jnp.maximum(0.0, 1.0 - (gap_along * gap_along + gap_across * gap_across) / (radius_cols * radius_cols)[None, :])
    weighted = spread * inverse[None, :]
    outer_terms = (weighted.T[:, :, None] * spread.T[:, None, :]).reshape(obs_total, members * members)
    drive_terms = (weighted * innovation[None, :]).T
    cross_terms = jnp.dot(taper_weights, outer_terms, precision=PRECISE, preferred_element_type=jnp.float32).reshape(-1, members, members)
    drive_sums = jnp.dot(taper_weights, drive_terms, precision=PRECISE, preferred_element_type=jnp.float32)
    identity = jnp.eye(members, dtype=jnp.float32)
    system = cross_terms + (members - 1.0) * identity
    norm_value = jnp.sqrt(lax.optimization_barrier(jnp.sum(system * system, axis=(1, 2))))
    iterate = system / norm_value[:, None, None]
    inv_root = jnp.broadcast_to(identity, system.shape)
    for sweep_index in range(NS_ITERS):
        update = 1.5 * identity - 0.5 * jnp.einsum('cij,cjk->cik', inv_root, iterate, precision=PRECISE)
        iterate = jnp.einsum('cij,cjk->cik', iterate, update, precision=PRECISE)
        inv_root = jnp.einsum('cij,cjk->cik', update, inv_root, precision=PRECISE)
    covariance = jnp.einsum('cij,cjk->cik', inv_root, inv_root, precision=PRECISE) / norm_value[:, None, None]
    mean_weights = jnp.einsum('cjk,ck->cj', covariance, drive_sums, precision=PRECISE)
    return jnp.sqrt((members - 1.0) / norm_value)[:, None, None] * inv_root + mean_weights[:, :, None]

def apply_weights(cell_stack_group, coarse_weights, later_weights):
    fraction = jnp.arange(4, dtype=jnp.float32) / 4.0
    blended = coarse_weights[:, :, None] * (1.0 - fraction)[None, None, :, None, None] + later_weights[:, :, None] * fraction[None, None, :, None, None]
    weight_shape = coarse_weights.shape
    fine_weights = blended.reshape(weight_shape[0], weight_shape[1] * 4, weight_shape[2], weight_shape[3])
    ensemble_mean = lax.optimization_barrier(jnp.sum(cell_stack_group, axis=0)) / cell_stack_group.shape[0]
    spread = cell_stack_group - ensemble_mean[None]
    return ensemble_mean[None] + jnp.einsum('jfxy,xyjk->kfxy', spread, fine_weights, precision=PRECISE)

def reference(background_fields, obs_col, measured_height, obs_radius, obs_value, obs_var):

    def evolve_replica(member_state):
        for time_step in range(FSTEPS):
            member_state = advance_grid(member_state)
        return member_state
    predicted_fields = lax.map(evolve_replica, background_fields)
    measured_easting = obs_col // NY
    measured_northing = obs_col % NY
    picked_readings = predicted_fields[:, measured_height, measured_easting, measured_northing]
    obs_mean = lax.optimization_barrier(jnp.sum(picked_readings, axis=0)) / MEMBERS
    obs_spread = picked_readings - obs_mean[None]
    innovation = obs_value - obs_mean
    inverse = 1.0 / obs_var

    def tile_analysis(patch_location_number):
        offsets = patch_location_number + jnp.arange(-1, 2, dtype=jnp.int32)
        neighbours = jnp.clip(offsets, 0, N_GX - 1)
        valid = ((offsets >= 0) & (offsets < N_GX)).astype(jnp.float32)
        spread = obs_spread.reshape(MEMBERS, N_GX, NOBS)[:, neighbours].reshape(MEMBERS, 3 * NOBS)
        near_innovation = innovation.reshape(N_GX, NOBS)[neighbours].reshape(-1)
        near_inverse = (inverse.reshape(N_GX, NOBS)[neighbours] * valid[:, None]).reshape(-1)
        near_along = measured_easting.reshape(N_GX, NOBS)[neighbours].reshape(-1)
        near_across = measured_northing.reshape(N_GX, NOBS)[neighbours].reshape(-1)
        near_radius = obs_radius.reshape(N_GX, NOBS)[neighbours].reshape(-1)
        coarse_count = NY // 4
        site_along = jnp.broadcast_to((patch_location_number * PATCH_CELLS_EAST + jnp.arange(PATCH_CELLS_EAST, dtype=jnp.int32))[:, None], (PATCH_CELLS_EAST, coarse_count)).reshape(-1)
        site_across = jnp.broadcast_to((4 * jnp.arange(coarse_count, dtype=jnp.int32))[None, :], (PATCH_CELLS_EAST, coarse_count)).reshape(-1)
        coarse = analysis_weights(spread, near_innovation, near_inverse, near_along, near_across, near_radius, site_along, site_across)
        coarse = coarse.reshape(PATCH_CELLS_EAST, coarse_count, MEMBERS, MEMBERS)
        later_weights = jnp.concatenate([coarse[:, 1:], coarse[:, -1:]], axis=1)
        patch_area = lax.dynamic_slice_in_dim(predicted_fields, patch_location_number * PATCH_CELLS_EAST, PATCH_CELLS_EAST, axis=2)
        return apply_weights(patch_area, coarse, later_weights)
    tiles_done = lax.map(tile_analysis, jnp.arange(N_GX, dtype=jnp.int32))
    return tiles_done.transpose(1, 2, 0, 3, 4).reshape(MEMBERS, FIELDS, NX, NY)
```

```python
import jax
import jax.numpy as jnp
from jax import lax
from jax.experimental import pallas as pl
from jax.experimental.pallas import tpu as pltpu
from jax.sharding import PartitionSpec as P

NS_ITERS = 6
COURANT = 0.6
DIFFUSE = 0.1
CHUNKS = 4
NS_PAIRS = 4
F32 = jnp.float32
BF16 = jnp.bfloat16
MESH = pl.DeviceIdType.MESH


def split2(x):
    hi = x.astype(BF16)
    lo = (x - hi.astype(F32)).astype(BF16)
    return hi, lo


def matmul(a, b):
    return lax.dot_general(a, b, (((1,), (0,)), ((), ())), preferred_element_type=F32)


def matmul_t(a, b):
    return lax.dot_general(a, b, (((1,), (1,)), ((), ())), preferred_element_type=F32)


def advance(west, center, east):
    shape = center.shape
    rows = center.reshape(-1, shape[-1])
    lane = lax.broadcasted_iota(jnp.int32, rows.shape, 1)
    south = jnp.where(lane == 0, 0.0, pltpu.roll(rows, 1, 1)).reshape(shape)
    north = jnp.where(lane == 127, 0.0, pltpu.roll(rows, 127, 1)).reshape(shape)
    return (
        center
        + COURANT * (west - center)
        + DIFFUSE * (west + east + south + north - 4.0 * center)
    )


def kernel(
    bg,
    col,
    radius,
    height,
    value,
    var,
    out,
    state,
    mid,
    fore,
    gathered,
    turned,
    weights,
    wgt,
    spread_ref,
    side,
    side_in,
    picked,
    stage,
    back,
    back_in,
    halo_send,
    halo_recv,
    side_send,
    side_recv,
    pick_send,
    pick_recv,
    fore_send,
    fore_recv,
    back_send,
    back_recv,
):
    me = lax.axis_index("member")
    tile = lax.axis_index("gx")
    group = 16
    tiles = lax.axis_size("gx")
    right = lax.rem(tile + 1, tiles)
    left = lax.rem(tile + tiles - 1, tiles)

    barrier = pltpu.get_barrier_semaphore()
    for other in (left, right):
        pl.semaphore_signal(barrier, inc=1, device_id={"gx": other}, device_id_type=MESH)

    def greet(d, carry):
        pl.semaphore_signal(
            barrier, inc=1, device_id={"member": lax.rem(me + d, group)}, device_id_type=MESH
        )
        return carry

    lax.fori_loop(1, group, greet, 0)

    def rearrange(x, carry):
        for k in range(4):
            rows = bg[pl.ds(k * 256 + x, 16, stride=16), :]
            for fh in range(4):
                state[x + 2, fh, 4 * k : 4 * k + 4, :] = rows[4 * fh : 4 * fh + 4]
        return carry

    lax.fori_loop(0, 16, rearrange, 0)
    pl.semaphore_wait(barrier, group - 1 + 2)

    def halo(direction, part):
        which = pl.ds(0, 1) if part == 0 else pl.ds(1, 3)
        src, dst, peer = ((16, 0, right), (2, 18, left))[direction]
        slot = direction * 2 + part
        return pltpu.make_async_remote_copy(
            src_ref=state.at[pl.ds(src, 2), which],
            dst_ref=state.at[pl.ds(dst, 2), which],
            send_sem=halo_send.at[slot],
            recv_sem=halo_recv.at[slot],
            device_id={"gx": peer},
            device_id_type=MESH,
        )

    for part in range(2):
        for direction in range(2):
            halo(direction, part).start()

    def first_step(index, which):
        mid[index, which] = advance(
            state[index, which], state[index + 1, which], state[index + 2, which]
        )

    def second_step(x, which):
        fore[x, which] = advance(mid[x, which], mid[x + 1, which], mid[x + 2, which])

    whole = pl.ds(0, 4)

    def inner_first(i, carry):
        first_step(i, whole)
        return carry

    def inner_second(i, carry):
        second_step(i, whole)
        return carry

    lax.fori_loop(2, 16, inner_first, 0)
    lax.fori_loop(2, 14, inner_second, 0)

    def outer_rows(part):
        which = pl.ds(0, 1) if part == 0 else pl.ds(1, 3)
        count = 1 if part == 0 else 3
        for direction in range(2):
            halo(direction, part).wait_recv()
        nothing = jnp.zeros((count, 16, 128), F32)

        @pl.when(tile == 0)
        def _():
            state[0, which] = nothing
            state[1, which] = nothing

        @pl.when(tile == tiles - 1)
        def _():
            state[18, which] = nothing
            state[19, which] = nothing

        for index in (0, 1, 16, 17):
            first_step(index, which)

        @pl.when(tile == 0)
        def _():
            mid[0, which] = nothing

        @pl.when(tile == tiles - 1)
        def _():
            mid[17, which] = nothing

        for x in (0, 1, 14, 15):
            second_step(x, which)

    outer_rows(0)

    def tile_row(ref, t):
        row = ref[pl.ds(t // 2, 1), :]
        return jnp.where(lax.rem(t, 2) == 0, row[:, :64], row[:, 64:])

    own_col = tile_row(col, tile)
    own_x = own_col // 128 - tile * 16
    own_y = lax.rem(own_col, 128)
    hot_y = (lax.broadcasted_iota(jnp.int32, (128, 64), 0) == own_y).astype(F32).astype(BF16)
    observed = fore[:, 0].reshape(256, 128)
    hi, lo = split2(observed)
    low = (observed - hi.astype(F32) - lo.astype(F32)).astype(BF16)
    along_y = (matmul(hi, hot_y) + matmul(lo, hot_y)) + matmul(low, hot_y)
    total = jnp.zeros((16, 64), F32)
    for x in range(16):
        total = total + jnp.where(own_x == x, along_y[16 * x : 16 * x + 16], 0.0)
    level = lax.rem(lax.broadcasted_iota(jnp.int32, (16, 64), 0), 4)
    total = jnp.where(level == height[...], total, 0.0)
    sampled = jnp.concatenate(
        [jnp.sum(total[4 * k : 4 * k + 4], axis=0, keepdims=True) for k in range(4)]
        + [value[...], var[...], jnp.zeros((2, 64), F32)],
        axis=0,
    )
    side[...] = jnp.concatenate([sampled, jnp.zeros((8, 64), F32)], axis=1)

    def to_side(direction):
        return pltpu.make_async_remote_copy(
            src_ref=side,
            dst_ref=side_in.at[direction],
            send_sem=side_send.at[direction],
            recv_sem=side_recv.at[direction],
            device_id={"gx": (right, left)[direction]},
            device_id_type=MESH,
        )

    for direction in range(2):
        to_side(direction).start()

    outer_rows(1)

    for direction in range(2):
        to_side(direction).wait_recv()
    from_left = side_in[0][:, :64]
    own = side[...][:, :64]
    from_right = side_in[1][:, :64]
    picked[me] = jnp.concatenate(
        [
            jnp.concatenate([from_left[:4], own[:4]], axis=1),
            jnp.concatenate([from_right[:4], jnp.zeros((4, 64), F32)], axis=1),
        ],
        axis=0,
    )

    def send_picked(d, peer, slot):
        return pltpu.make_async_remote_copy(
            src_ref=picked.at[slot],
            dst_ref=picked.at[slot],
            send_sem=pick_send.at[d],
            recv_sem=pick_recv.at[slot],
            device_id={"member": peer},
            device_id_type=MESH,
        )

    def send_fore(d, peer, slot):
        return pltpu.make_async_remote_copy(
            src_ref=fore.at[peer],
            dst_ref=gathered.at[:, pl.ds(pl.multiple_of(slot * 16, 16), 16), :],
            send_sem=fore_send.at[d],
            recv_sem=fore_recv.at[slot],
            device_id={"member": peer},
            device_id_type=MESH,
        )

    def over_peers(action):
        def body(d, carry):
            action(d, lax.rem(me + d, group))
            return carry

        lax.fori_loop(1, group, body, 0)

    over_peers(lambda d, peer: send_picked(d, peer, me).start())
    over_peers(lambda d, peer: send_fore(d, peer, me).start())
    gathered[:, pl.ds(pl.multiple_of(me * 16, 16), 16), :] = fore[me]

    def three(a, b, c, fill):
        return jnp.concatenate([a, b, c, jnp.full((1, 64), fill, a.dtype)], axis=1)

    before = jnp.maximum(tile - 1, 0)
    after = jnp.minimum(tile + 1, tiles - 1)
    near_col = three(tile_row(col, before), own_col, tile_row(col, after), 0)
    near_radius = three(
        tile_row(radius, before), tile_row(radius, tile), tile_row(radius, after), 1
    ).astype(F32)
    near_value = three(from_left[4:5], own[4:5], from_right[4:5], 0.0)
    near_var = three(from_left[5:6], own[5:6], from_right[5:6], 1.0)
    lane = lax.broadcasted_iota(jnp.int32, (1, 256), 1)
    first = jnp.where(tile == 0, 64, 0)
    last = jnp.where(tile == tiles - 1, 128, 192)
    valid = (lane >= first) & (lane < last)
    inverse = jnp.where(valid, 1.0 / near_var, 0.0)
    gap_along = (tile * 16 + me - near_col // 128).astype(F32)
    site = 4 * lax.broadcasted_iota(jnp.int32, (32, 256), 0)
    gap_across = (site - lax.rem(near_col, 128)).astype(F32)
    taper = jnp.maximum(
        0.0,
        1.0 - (gap_along * gap_along + gap_across * gap_across) / (near_radius * near_radius),
    )
    wgt[...] = taper * inverse

    over_peers(lambda d, peer: send_picked(d, peer, peer).wait_recv())
    ensemble = jnp.concatenate(
        [
            jnp.concatenate([picked[m][:4] for m in range(16)], axis=0),
            jnp.concatenate([picked[m][4:] for m in range(16)], axis=0),
        ],
        axis=1,
    )
    mean = jnp.sum(ensemble, axis=0, keepdims=True) / 64.0
    spread = ensemble - mean
    innovation = near_value - mean
    spread_ref[...] = spread
    spread_hi, spread_lo = split2(spread)
    across_obs = jnp.concatenate([spread_hi, spread_hi, spread_lo, spread_lo], axis=0)

    lane2 = lax.broadcasted_iota(jnp.int32, (64, 128), 1)
    row2 = lax.broadcasted_iota(jnp.int32, (64, 128), 0)
    is_first = lane2 < 64
    eye = (lax.rem(lane2, 64) == row2).astype(F32)
    is_first_row = lax.broadcasted_iota(jnp.int32, (1, 128), 1) < 64

    def operand(x):
        hi, lo = split2(x)
        return jnp.concatenate([hi, lo], axis=1)

    def stationary(x):
        hi = x.astype(BF16).astype(F32)
        lo = x - hi
        zero = jnp.zeros_like(x)
        top = jnp.concatenate(
            [jnp.where(is_first, hi, zero), jnp.where(is_first, lo, zero)], axis=1
        ).astype(BF16)
        bottom = jnp.concatenate(
            [jnp.where(is_first, zero, hi), jnp.where(is_first, zero, lo)], axis=1
        ).astype(BF16)
        return jnp.concatenate([top, bottom, top, bottom], axis=0)

    def fold(x):
        return x[:, :128] + x[:, 128:]

    def solve(batch, carry):
        pairs = [batch * NS_PAIRS + i for i in range(NS_PAIRS)]
        system, drive = [], []
        for p in pairs:
            scaled = [spread_ref[...] * wgt[pl.ds(2 * p + h, 1), :] for h in range(2)]
            both = jnp.concatenate(scaled, axis=0)
            hi, lo = split2(both)
            product = fold(matmul_t(hi, across_obs)) + matmul_t(lo, across_obs[:128])
            system.append(jnp.where(is_first, product[:64], product[64:]) + 63.0 * eye)
            sums = [jnp.sum(s * innovation, axis=1, keepdims=True) for s in scaled]
            drive.append(jnp.where(is_first, sums[0], sums[1]))
        inv_norm, power, root = [], [], []
        for s in system:
            squares = jnp.sum(s * s, axis=0, keepdims=True)
            one = jnp.sum(jnp.where(is_first_row, squares, 0.0), axis=1, keepdims=True)
            two = jnp.sum(jnp.where(is_first_row, 0.0, squares), axis=1, keepdims=True)
            inv = 1.0 / jnp.sqrt(jnp.where(is_first_row, one, two))
            inv_norm.append(inv)
            power.append(s * inv)
        root = [1.5 * eye - 0.5 * p for p in power]
        for sweep in range(NS_ITERS - 1):
            fixed = [stationary(p) for p in power]
            moving = [operand(p) for p in power]
            if sweep == 0:
                square = [fold(matmul(m, f)) for m, f in zip(moving, fixed)]
            else:
                stacked = [
                    fold(matmul(jnp.concatenate([m, operand(z)], axis=0), f))
                    for m, z, f in zip(moving, root, fixed)
                ]
                square = [s[:64] for s in stacked]
                root = [1.5 * z - 0.5 * s[64:] for z, s in zip(root, stacked)]
            cube = [fold(matmul(operand(s), f)) for s, f in zip(square, fixed)]
            power = [2.25 * p - 1.5 * s + 0.25 * c for p, s, c in zip(power, square, cube)]
        root = [
            1.5 * z - 0.5 * fold(matmul(operand(z), stationary(p))) for z, p in zip(root, power)
        ]
        for p, z, inv, d in zip(pairs, root, inv_norm, drive):
            through = jnp.sum(z * d, axis=0, keepdims=True)
            again = z * through
            one = jnp.sum(jnp.where(is_first, again, 0.0), axis=1, keepdims=True)
            two = jnp.sum(jnp.where(is_first, 0.0, again), axis=1, keepdims=True)
            w = jnp.sqrt(63.0 * inv) * z + jnp.where(is_first, one, two) * inv
            w = w + (1.0 - jnp.sum(w, axis=0, keepdims=True)) * (1.0 / 64.0)
            hi = w.astype(BF16).astype(F32)
            lo = w - hi
            weights[2 * p] = jnp.where(is_first, hi, pltpu.roll(lo, 64, 1)).astype(BF16)
            weights[2 * p + 1] = jnp.where(is_first, pltpu.roll(hi, 64, 1), lo).astype(BF16)
        return carry

    lax.fori_loop(0, 16 // NS_PAIRS, solve, 0)
    weights[32] = weights[31]
    weights[33] = jnp.zeros((64, 128), BF16)

    over_peers(lambda d, peer: send_fore(d, peer, peer).wait_recv())

    def turn(fh, carry):
        for fl in range(4):
            rows = gathered[fh, pl.ds(fl, 64, stride=4), :]
            turned[fh * 4 + fl] = jnp.concatenate([rows, rows], axis=0).T
        return carry

    lax.fori_loop(0, 4, turn, 0)

    y8 = lax.broadcasted_iota(jnp.int32, (1, 8, 128), 1).astype(F32) * 0.25
    half = lax.broadcasted_iota(jnp.int32, (1, 8, 128), 2) < 64
    tent = [jnp.maximum(0.0, 1.0 - jnp.abs(y8 - c)) for c in range(3)]
    coef_a = jnp.where(half, tent[0], tent[1])
    coef_b = jnp.where(half, tent[2], 0.0)

    def send_back(q, d, peer, slot):
        return pltpu.make_async_remote_copy(
            src_ref=back.at[q, pl.ds(pl.multiple_of(peer * 16, 16), 16), :],
            dst_ref=back_in.at[q, slot],
            send_sem=back_send.at[q, d],
            recv_sem=back_recv.at[q, slot],
            device_id={"member": peer},
            device_id_type=MESH,
        )

    def apply(step, carry):
        q = CHUNKS - 1 - step
        for part in range(4):
            block = q * 4 + part
            rows = turned[:, pl.ds(pl.multiple_of(block * 8, 8), 8), :]
            near = operand((rows * coef_a).reshape(128, 128))
            far = operand((rows * coef_b).reshape(128, 128))
            c01 = weights[pl.ds(2 * block, 2)].reshape(128, 128)
            c23 = weights[pl.ds(2 * block + 2, 2)].reshape(128, 128)
            product = matmul(near, jnp.concatenate([c01, c01], axis=0)) + matmul(
                far, jnp.concatenate([c23, c23], axis=0)
            )
            product = (product[:, :64] + product[:, 64:]).reshape(4, 4, 8, 64)
            for fl in range(4):
                stage[:, fl * 32 + part * 8 : fl * 32 + part * 8 + 8, :] = product[:, fl]
        for fh in range(4):
            back[q, pl.ds(fh, 64, stride=4), :] = stage[fh].T
        over_peers(lambda d, peer: send_back(q, d, peer, me).start())
        back_in[q, me] = back[q, pl.ds(pl.multiple_of(me * 16, 16), 16), :]
        return carry

    lax.fori_loop(0, CHUNKS, apply, 0)

    for part in range(2):
        for direction in range(2):
            halo(direction, part).wait_send()
    for direction in range(2):
        to_side(direction).wait_send()
    over_peers(lambda d, peer: send_picked(d, peer, me).wait_send())
    over_peers(lambda d, peer: send_fore(d, peer, me).wait_send())
    for q in range(CHUNKS - 1, -1, -1):
        over_peers(lambda d, peer, q=q: send_back(q, d, peer, me).wait_send())
        over_peers(lambda d, peer, q=q: send_back(q, d, peer, peer).wait_recv())

    lane16 = lax.broadcasted_iota(jnp.int32, (16, 128), 1)

    def place(x, carry):
        chunks = [back_in[q, x] for q in range(4)]
        for fl in range(4):
            moved = [
                chunks[q] if q == fl else pltpu.roll(chunks[q], ((q - fl) * 32) % 128, 1)
                for q in range(4)
            ]
            low_half = jnp.where(lane16 < 32, moved[0], moved[1])
            high_half = jnp.where(lane16 < 96, moved[2], moved[3])
            out[pl.ds(fl * 16 + x, 16, stride=64), :] = jnp.where(
                lane16 < 64, low_half, high_half
            )
        return carry

    lax.fori_loop(0, 16, place, 0)


def per_device(background_fields, obs_col, measured_height, obs_radius, obs_value, obs_var):
    dma = pltpu.SemaphoreType.DMA
    result = pl.pallas_call(
        kernel,
        out_shape=jax.ShapeDtypeStruct((1024, 128), F32),
        in_specs=[pl.BlockSpec(memory_space=pltpu.VMEM)] * 6,
        out_specs=pl.BlockSpec(memory_space=pltpu.VMEM),
        scratch_shapes=[
            pltpu.VMEM((20, 4, 16, 128), F32),
            pltpu.VMEM((18, 4, 16, 128), F32),
            pltpu.VMEM((16, 4, 16, 128), F32),
            pltpu.VMEM((4, 256, 128), F32),
            pltpu.VMEM((16, 128, 128), F32),
            pltpu.VMEM((34, 64, 128), BF16),
            pltpu.VMEM((32, 256), F32),
            pltpu.VMEM((64, 256), F32),
            pltpu.VMEM((8, 128), F32),
            pltpu.VMEM((2, 8, 128), F32),
            pltpu.VMEM((16, 8, 128), F32),
            pltpu.VMEM((4, 128, 64), F32),
            pltpu.VMEM((CHUNKS, 256, 128), F32),
            pltpu.VMEM((CHUNKS, 16, 16, 128), F32),
            dma((4,)),
            dma((4,)),
            dma((2,)),
            dma((2,)),
            dma((16,)),
            dma((16,)),
            dma((16,)),
            dma((16,)),
            dma((CHUNKS, 16)),
            dma((CHUNKS, 16)),
        ],
        compiler_params=pltpu.CompilerParams(
            collective_id=0, has_side_effects=True, vmem_limit_bytes=40 * 1024 * 1024
        ),
    )(
        background_fields.reshape(1024, 128),
        obs_col.reshape(16, 128),
        obs_radius.reshape(16, 128),
        measured_height.reshape(1, 64),
        obs_value.reshape(1, 64),
        obs_var.reshape(1, 64),
    )
    return result.reshape(4, 16, 16, 128)


def solution(mesh):
    return jax.shard_map(
        per_device,
        mesh=mesh,
        in_specs=(P("member", None, "gx", None), P(), P("gx"), P(), P("gx"), P("gx")),
        out_specs=P("member", None, "gx", None),
        check_vma=False,
    )
```

```python
import jax
import jax.numpy as jnp
from jax import lax
from jax.experimental import pallas as pl
from jax.experimental.pallas import tpu as pltpu
from jax.sharding import PartitionSpec as P

NS_ITERS = 6
COURANT = 0.6
DIFFUSE = 0.1
CHUNKS = 4
NS_PAIRS = 4
EARLY = 6
F32 = jnp.float32
BF16 = jnp.bfloat16
MESH = pl.DeviceIdType.MESH


def split2(x):
    hi = x.astype(BF16)
    lo = (x - hi.astype(F32)).astype(BF16)
    return hi, lo


def matmul(a, b):
    return lax.dot_general(a, b, (((1,), (0,)), ((), ())), preferred_element_type=F32)


def matmul_t(a, b):
    return lax.dot_general(a, b, (((1,), (1,)), ((), ())), preferred_element_type=F32)


def advance(west, center, east):
    shape = center.shape
    rows = center.reshape(-1, shape[-1])
    lane = lax.broadcasted_iota(jnp.int32, rows.shape, 1)
    south = jnp.where(lane == 0, 0.0, pltpu.roll(rows, 1, 1)).reshape(shape)
    north = jnp.where(lane == 127, 0.0, pltpu.roll(rows, 127, 1)).reshape(shape)
    return (
        center
        + COURANT * (west - center)
        + DIFFUSE * (west + east + south + north - 4.0 * center)
    )


def kernel(
    bg_hbm,
    col_hbm,
    radius_hbm,
    height_hbm,
    value_hbm,
    var_hbm,
    back_in,
    bg,
    col,
    radius,
    height,
    value,
    var,
    state,
    mid,
    fore,
    gathered,
    turned,
    weights,
    wgt,
    spread_ref,
    side,
    side_in,
    picked,
    picked_in,
    stage,
    back,
    load_sem,
    halo_send,
    halo_recv,
    side_send,
    side_recv,
    pick_send,
    pick_recv,
    fore_send,
    fore_recv,
    back_send,
    back_recv,
    keep_sem,
):
    me = lax.axis_index("member")
    tile = lax.axis_index("gx")
    group = 16
    tiles = lax.axis_size("gx")
    right = lax.rem(tile + 1, tiles)
    left = lax.rem(tile + tiles - 1, tiles)

    def load(i):
        pairs = (
            (bg_hbm, bg),
            (value_hbm, value),
            (var_hbm, var),
            (col_hbm, col),
            (height_hbm, height),
            (radius_hbm, radius),
        )
        return pltpu.make_async_copy(*pairs[i], load_sem.at[i])

    for i in range(6):
        load(i).start()

    barrier = pltpu.get_barrier_semaphore()

    def over_three(action):
        def body(d, carry):
            peer = lax.rem(me + d, group)
            action(0, d, {"member": peer, "gx": right})
            action(2, d, {"member": peer, "gx": left})

            @pl.when(d > 0)
            def _():
                action(1, d, {"member": peer})

            return carry

        lax.fori_loop(0, group, body, 0)

    over_three(
        lambda rel, d, device: pl.semaphore_signal(
            barrier, inc=1, device_id=device, device_id_type=MESH
        )
    )
    for i in range(6):
        load(i).wait()

    def rearrange(x, carry):
        for k in range(4):
            rows = bg[pl.ds(k * 256 + x, 16, stride=16), :]
            for fh in range(4):
                state[x + 2, fh, 4 * k : 4 * k + 4, :] = rows[4 * fh : 4 * fh + 4]
        return carry

    lax.fori_loop(0, 16, rearrange, 0)
    side[...] = jnp.concatenate(
        [
            jnp.concatenate([value[...], var[...]], axis=1),
            jnp.zeros((7, 128), F32),
        ],
        axis=0,
    )
    pl.semaphore_wait(barrier, 3 * group - 1)

    def halo(direction, part):
        which = pl.ds(0, 1) if part == 0 else pl.ds(1, 3)
        src, dst, peer = ((16, 0, right), (2, 18, left))[direction]
        slot = direction * 2 + part
        return pltpu.make_async_remote_copy(
            src_ref=state.at[pl.ds(src, 2), which],
            dst_ref=state.at[pl.ds(dst, 2), which],
            send_sem=halo_send.at[slot],
            recv_sem=halo_recv.at[slot],
            device_id={"gx": peer},
            device_id_type=MESH,
        )

    def to_side(direction):
        return pltpu.make_async_remote_copy(
            src_ref=side,
            dst_ref=side_in.at[direction],
            send_sem=side_send.at[direction],
            recv_sem=side_recv.at[direction],
            device_id={"gx": (right, left)[direction]},
            device_id_type=MESH,
        )

    for direction in range(2):
        halo(direction, 0).start()
    for direction in range(2):
        to_side(direction).start()
    for direction in range(2):
        halo(direction, 1).start()

    def first_step(index, which):
        mid[index, which] = advance(
            state[index, which], state[index + 1, which], state[index + 2, which]
        )

    def second_step(x, which):
        fore[x, which] = advance(mid[x, which], mid[x + 1, which], mid[x + 2, which])

    whole = pl.ds(0, 4)

    def inner_first(i, carry):
        for j in range(7):
            first_step(2 + 7 * i + j, whole)
        return carry

    def inner_second(i, carry):
        for j in range(6):
            second_step(2 + 6 * i + j, whole)
        return carry

    lax.fori_loop(0, 2, inner_first, 0)
    lax.fori_loop(0, 2, inner_second, 0)

    def send_fore(d, peer, slot):
        return pltpu.make_async_remote_copy(
            src_ref=fore.at[peer],
            dst_ref=gathered.at[:, pl.ds(pl.multiple_of(slot * 16, 16), 16), :],
            send_sem=fore_send.at[d],
            recv_sem=fore_recv.at[slot],
            device_id={"member": peer},
            device_id_type=MESH,
        )

    def over_peers(action):
        def body(d, carry):
            action(d, lax.rem(me + d, group))
            return carry

        lax.fori_loop(1, group, body, 0)

    def start_fore(turn):
        def body(d, peer):
            inner = (peer >= 2) & (peer < 14)
            early = inner & (d <= EARLY)
            now = (early, inner & (d > EARLY), jnp.logical_not(inner))[turn]

            @pl.when(now)
            def _():
                send_fore(d, peer, me).start()

        over_peers(body)

    start_fore(0)

    def outer_rows(part):
        which = pl.ds(0, 1) if part == 0 else pl.ds(1, 3)
        count = 1 if part == 0 else 3
        for direction in range(2):
            halo(direction, part).wait_recv()
        nothing = jnp.zeros((count, 16, 128), F32)

        @pl.when(tile == 0)
        def _():
            state[0, which] = nothing
            state[1, which] = nothing

        @pl.when(tile == tiles - 1)
        def _():
            state[18, which] = nothing
            state[19, which] = nothing

        for index in (0, 1, 16, 17):
            first_step(index, which)

        @pl.when(tile == 0)
        def _():
            mid[0, which] = nothing

        @pl.when(tile == tiles - 1)
        def _():
            mid[17, which] = nothing

        for x in (0, 1, 14, 15):
            second_step(x, which)

    outer_rows(0)

    def tile_row(ref, t):
        row = ref[pl.ds(t // 2, 1), :]
        return jnp.where(lax.rem(t, 2) == 0, row[:, :64], row[:, 64:])

    own_col = tile_row(col, tile)
    own_x = own_col // 128 - tile * 16
    own_y = lax.rem(own_col, 128)
    hot_y = (lax.broadcasted_iota(jnp.int32, (128, 64), 0) == own_y).astype(F32).astype(BF16)
    observed = fore[:, 0].reshape(256, 128)
    hi, lo = split2(observed)
    low = (observed - hi.astype(F32) - lo.astype(F32)).astype(BF16)
    along_y = (matmul(hi, hot_y) + matmul(lo, hot_y)) + matmul(low, hot_y)
    total = jnp.zeros((16, 64), F32)
    for x in range(16):
        total = total + jnp.where(own_x == x, along_y[16 * x : 16 * x + 16], 0.0)
    level = lax.rem(lax.broadcasted_iota(jnp.int32, (16, 64), 0), 4)
    total = jnp.where(level == height[...], total, 0.0)
    sums = [jnp.sum(total[4 * k : 4 * k + 4], axis=0, keepdims=True) for k in range(4)]
    picked[...] = jnp.concatenate(
        [
            jnp.concatenate([sums[0], sums[1]], axis=1),
            jnp.concatenate([sums[2], sums[3]], axis=1),
        ],
        axis=0,
    )

    def send_picked(rel, d, device):
        return pltpu.make_async_remote_copy(
            src_ref=picked,
            dst_ref=picked_in.at[rel, me],
            send_sem=pick_send.at[rel, d],
            recv_sem=pick_recv.at[rel],
            device_id=device,
            device_id_type=MESH,
        )

    over_three(lambda rel, d, device: send_picked(rel, d, device).start())
    picked_in[1, me] = picked[...]
    start_fore(1)

    outer_rows(1)
    start_fore(2)
    gathered[:, pl.ds(pl.multiple_of(me * 16, 16), 16), :] = fore[me]

    def three(a, b, c, fill):
        return jnp.concatenate([a, b, c, jnp.full((1, 64), fill, a.dtype)], axis=1)

    before = jnp.maximum(tile - 1, 0)
    after = jnp.minimum(tile + 1, tiles - 1)
    near_col = three(tile_row(col, before), own_col, tile_row(col, after), 0)
    near_radius = three(
        tile_row(radius, before), tile_row(radius, tile), tile_row(radius, after), 1
    ).astype(F32)
    for direction in range(2):
        to_side(direction).wait_recv()
    from_left, own, from_right = side_in[0, 0:1, :], side[0:1, :], side_in[1, 0:1, :]
    near_value = three(from_left[:, :64], own[:, :64], from_right[:, :64], 0.0)
    near_var = three(from_left[:, 64:], own[:, 64:], from_right[:, 64:], 1.0)
    lane = lax.broadcasted_iota(jnp.int32, (1, 256), 1)
    first = jnp.where(tile == 0, 64, 0)
    last = jnp.where(tile == tiles - 1, 128, 192)
    valid = (lane >= first) & (lane < last)
    inverse = jnp.where(valid, 1.0 / near_var, 0.0)
    gap_along = (tile * 16 + me - near_col // 128).astype(F32)
    site = 4 * lax.broadcasted_iota(jnp.int32, (32, 256), 0)
    gap_across = (site - lax.rem(near_col, 128)).astype(F32)
    taper = jnp.maximum(
        0.0,
        1.0 - (gap_along * gap_along + gap_across * gap_across) / (near_radius * near_radius),
    )
    wgt[...] = taper * inverse

    def arrived(rel):
        count = 15 if rel == 1 else 16
        pltpu.make_async_copy(
            picked_in.at[rel, pl.ds(0, count)],
            picked_in.at[rel, pl.ds(0, count)],
            pick_recv.at[rel],
        ).wait()

    def by_member(rel):
        rows = jnp.concatenate([picked_in[rel, m] for m in range(16)], axis=0)
        return jnp.concatenate([rows[:, :64], rows[:, 64:]], axis=0)

    for rel in range(3):
        arrived(rel)
    ensemble = jnp.concatenate(
        [by_member(rel) for rel in range(3)] + [jnp.zeros((64, 64), F32)], axis=1
    )
    mean = jnp.sum(ensemble, axis=0, keepdims=True) / 64.0
    spread = ensemble - mean
    innovation = near_value - mean
    spread_ref[...] = spread
    spread_hi, spread_lo = split2(spread)
    across_obs = jnp.concatenate([spread_hi, spread_hi, spread_lo, spread_lo], axis=0)

    lane2 = lax.broadcasted_iota(jnp.int32, (64, 128), 1)
    row2 = lax.broadcasted_iota(jnp.int32, (64, 128), 0)
    is_first = lane2 < 64
    eye = (lax.rem(lane2, 64) == row2).astype(F32)
    is_first_row = lax.broadcasted_iota(jnp.int32, (1, 128), 1) < 64

    def operand(x):
        hi, lo = split2(x)
        return jnp.concatenate([hi, lo], axis=1)

    def stationary(x):
        hi = x.astype(BF16).astype(F32)
        lo = x - hi
        zero = jnp.zeros_like(x)
        top = jnp.concatenate(
            [jnp.where(is_first, hi, zero), jnp.where(is_first, lo, zero)], axis=1
        ).astype(BF16)
        bottom = jnp.concatenate(
            [jnp.where(is_first, zero, hi), jnp.where(is_first, zero, lo)], axis=1
        ).astype(BF16)
        return jnp.concatenate([top, bottom, top, bottom], axis=0)

    def fold(x):
        return x[:, :128] + x[:, 128:]

    def solve(batch):
        pairs = [batch * NS_PAIRS + i for i in range(NS_PAIRS)]
        system, drive = [], []
        for p in pairs:
            scaled = [spread_ref[...] * wgt[pl.ds(2 * p + h, 1), :] for h in range(2)]
            both = jnp.concatenate(scaled, axis=0)
            hi, lo = split2(both)
            product = fold(matmul_t(hi, across_obs)) + matmul_t(lo, across_obs[:128])
            system.append(jnp.where(is_first, product[:64], product[64:]) + 63.0 * eye)
            sums = [jnp.sum(s * innovation, axis=1, keepdims=True) for s in scaled]
            drive.append(jnp.where(is_first, sums[0], sums[1]))
        inv_norm, power, root = [], [], []
        for s in system:
            squares = jnp.sum(s * s, axis=0, keepdims=True)
            one = jnp.sum(jnp.where(is_first_row, squares, 0.0), axis=1, keepdims=True)
            two = jnp.sum(jnp.where(is_first_row, 0.0, squares), axis=1, keepdims=True)
            inv = 1.0 / jnp.sqrt(jnp.where(is_first_row, one, two))
            inv_norm.append(inv)
            power.append(s * inv)
        root = [1.5 * eye - 0.5 * p for p in power]
        for sweep in range(NS_ITERS - 1):
            fixed = [stationary(p) for p in power]
            moving = [operand(p) for p in power]
            if sweep == 0:
                square = [fold(matmul(m, f)) for m, f in zip(moving, fixed)]
            else:
                stacked = [
                    fold(matmul(jnp.concatenate([m, operand(z)], axis=0), f))
                    for m, z, f in zip(moving, root, fixed)
                ]
                square = [s[:64] for s in stacked]
                root = [1.5 * z - 0.5 * s[64:] for z, s in zip(root, stacked)]
            cube = [fold(matmul(operand(s), f)) for s, f in zip(square, fixed)]
            power = [2.25 * p - 1.5 * s + 0.25 * c for p, s, c in zip(power, square, cube)]
        root = [
            1.5 * z - 0.5 * fold(matmul(operand(z), stationary(p))) for z, p in zip(root, power)
        ]
        for p, z, inv, d in zip(pairs, root, inv_norm, drive):
            through = jnp.sum(z * d, axis=0, keepdims=True)
            again = z * through
            one = jnp.sum(jnp.where(is_first, again, 0.0), axis=1, keepdims=True)
            two = jnp.sum(jnp.where(is_first, 0.0, again), axis=1, keepdims=True)
            w = jnp.sqrt(63.0 * inv) * z + jnp.where(is_first, one, two) * inv
            w = w + (1.0 - jnp.sum(w, axis=0, keepdims=True)) * (1.0 / 64.0)
            hi = w.astype(BF16).astype(F32)
            lo = w - hi
            weights[2 * p] = jnp.where(is_first, hi, pltpu.roll(lo, 64, 1)).astype(BF16)
            weights[2 * p + 1] = jnp.where(is_first, pltpu.roll(hi, 64, 1), lo).astype(BF16)


    def turn(fh, carry):
        for fl in range(4):
            rows = jnp.concatenate(
                [gathered[fh, pl.ds(fl + 4 * odd, 32, stride=8), :] for odd in range(2)], axis=0
            )
            turned[fh * 4 + fl] = jnp.concatenate([rows, rows], axis=0).T
        return carry


    y8 = lax.broadcasted_iota(jnp.int32, (1, 8, 128), 1).astype(F32) * 0.25
    half = lax.broadcasted_iota(jnp.int32, (1, 8, 128), 2) < 64
    tent = [jnp.maximum(0.0, 1.0 - jnp.abs(y8 - c)) for c in range(3)]
    coef_a = jnp.where(half, tent[0], tent[1])
    coef_b = jnp.where(half, tent[2], 0.0)

    def send_back(q, d, peer, slot):
        return pltpu.make_async_remote_copy(
            src_ref=back.at[q, pl.ds(pl.multiple_of(peer * 16, 16), 16), :],
            dst_ref=back_in.at[q, slot],
            send_sem=back_send.at[q, d],
            recv_sem=back_recv.at[q, slot],
            device_id={"member": peer},
            device_id_type=MESH,
        )

    def keep(q):
        return pltpu.make_async_copy(
            back.at[q, pl.ds(pl.multiple_of(me * 16, 16), 16), :],
            back_in.at[q, me],
            keep_sem.at[q],
        )

    def chunk(step, carry):
        q = CHUNKS - 1 - step
        solve(q)

        @pl.when(step == 0)
        def _():
            weights[32] = weights[31]
            weights[33] = jnp.zeros((64, 128), BF16)
            over_peers(lambda d, peer: send_fore(d, peer, peer).wait_recv())
            lax.fori_loop(0, 4, turn, 0)

        for part in range(4):
            block = q * 4 + part
            rows = turned[:, pl.ds(pl.multiple_of(block * 8, 8), 8), :]
            near = operand((rows * coef_a).reshape(128, 128))
            far = operand((rows * coef_b).reshape(128, 128))
            c01 = weights[pl.ds(2 * block, 2)].reshape(128, 128)
            c23 = weights[pl.ds(2 * block + 2, 2)].reshape(128, 128)
            product = matmul(near, jnp.concatenate([c01, c01], axis=0)) + matmul(
                far, jnp.concatenate([c23, c23], axis=0)
            )
            product = (product[:, :64] + product[:, 64:]).reshape(4, 4, 8, 64)
            for fl in range(4):
                stage[:, fl * 32 + part * 8 : fl * 32 + part * 8 + 8, :] = product[:, fl]
        for fh in range(4):
            rows = stage[fh].T
            for odd in range(2):
                back[q, pl.ds(fh + 4 * odd, 32, stride=8), :] = rows[32 * odd : 32 * odd + 32]
        over_peers(lambda d, peer: send_back(q, d, peer, me).start())
        keep(q).start()
        return carry

    lax.fori_loop(0, CHUNKS, chunk, 0)

    for part in range(2):
        for direction in range(2):
            halo(direction, part).wait_send()
    for direction in range(2):
        to_side(direction).wait_send()
    over_three(lambda rel, d, device: send_picked(rel, d, device).wait_send())
    over_peers(lambda d, peer: send_fore(d, peer, me).wait_send())
    for q in range(CHUNKS - 1, -1, -1):
        over_peers(lambda d, peer, q=q: send_back(q, d, peer, me).wait_send())
        over_peers(lambda d, peer, q=q: send_back(q, d, peer, peer).wait_recv())
        keep(q).wait()


def place(back_in, out, landed, placed, load_sem, leave_sem):
    lane = lax.broadcasted_iota(jnp.int32, (16, 128), 1)
    flat = placed.reshape(2, 512, 128)

    def load(part):
        rows = pl.ds(4 * part, 4)
        return pltpu.make_async_copy(back_in.at[:, rows], landed.at[:, rows], load_sem.at[part])

    def leave(half):
        return pltpu.make_async_copy(
            placed.at[half], out.at[:, :, pl.ds(8 * half, 8), :], leave_sem.at[half]
        )

    for part in range(4):
        load(part).start()
    for half in range(2):
        for x in range(8):
            if x % 4 == 0:
                load(2 * half + x // 4).wait()
            chunks = [landed[q, 8 * half + x] for q in range(4)]
            for fl in range(4):
                moved = [
                    chunks[q] if q == fl else pltpu.roll(chunks[q], ((q - fl) * 32) % 128, 1)
                    for q in range(4)
                ]
                low_half = jnp.where(lane < 32, moved[0], moved[1])
                high_half = jnp.where(lane < 96, moved[2], moved[3])
                flat[half, pl.ds(fl * 8 + x, 16, stride=32), :] = jnp.where(
                    lane < 64, low_half, high_half
                )
        leave(half).start()
    for half in range(2):
        leave(half).wait()


def per_device(background_fields, obs_col, measured_height, obs_radius, obs_value, obs_var):
    dma = pltpu.SemaphoreType.DMA
    result = pl.pallas_call(
        kernel,
        out_shape=jax.ShapeDtypeStruct((CHUNKS, 16, 16, 128), F32),
        in_specs=[pl.BlockSpec(memory_space=pltpu.HBM)] * 6,
        out_specs=pl.BlockSpec(memory_space=pltpu.HBM),
        scratch_shapes=[
            pltpu.VMEM((1024, 128), F32),
            pltpu.VMEM((16, 128), jnp.int32),
            pltpu.VMEM((16, 128), jnp.int32),
            pltpu.VMEM((1, 64), jnp.int32),
            pltpu.VMEM((1, 64), F32),
            pltpu.VMEM((1, 64), F32),
            pltpu.VMEM((20, 4, 16, 128), F32),
            pltpu.VMEM((18, 4, 16, 128), F32),
            pltpu.VMEM((16, 4, 16, 128), F32),
            pltpu.VMEM((4, 256, 128), F32),
            pltpu.VMEM((16, 128, 128), F32),
            pltpu.VMEM((34, 64, 128), BF16),
            pltpu.VMEM((32, 256), F32),
            pltpu.VMEM((64, 256), F32),
            pltpu.VMEM((8, 128), F32),
            pltpu.VMEM((2, 8, 128), F32),
            pltpu.VMEM((2, 128), F32),
            pltpu.VMEM((3, 16, 2, 128), F32),
            pltpu.VMEM((4, 128, 64), F32),
            pltpu.VMEM((CHUNKS, 256, 128), F32),
            dma((6,)),
            dma((4,)),
            dma((4,)),
            dma((2,)),
            dma((2,)),
            dma((3, 16)),
            dma((3,)),
            dma((16,)),
            dma((16,)),
            dma((CHUNKS, 16)),
            dma((CHUNKS, 16)),
            dma((CHUNKS,)),
        ],
        compiler_params=pltpu.CompilerParams(
            collective_id=0, has_side_effects=True, vmem_limit_bytes=64 * 1024 * 1024
        ),
    )(
        *(
            pltpu.with_memory_space_constraint(x, pltpu.HBM)
            for x in (
                background_fields.reshape(1024, 128),
                obs_col.reshape(16, 128),
                obs_radius.reshape(16, 128),
                measured_height.reshape(1, 64),
                obs_value.reshape(1, 64),
                obs_var.reshape(1, 64),
            )
        )
    )
    return pl.pallas_call(
        place,
        out_shape=jax.ShapeDtypeStruct((4, 16, 16, 128), F32),
        in_specs=[pl.BlockSpec(memory_space=pltpu.HBM)],
        out_specs=pl.BlockSpec(memory_space=pltpu.HBM),
        scratch_shapes=[
            pltpu.VMEM((CHUNKS, 16, 16, 128), F32),
            pltpu.VMEM((2, 4, 16, 8, 128), F32),
            dma((4,)),
            dma((2,)),
        ],
        compiler_params=pltpu.CompilerParams(vmem_limit_bytes=60 * 1024 * 1024),
    )(result)


def solution(mesh):
    return jax.shard_map(
        per_device,
        mesh=mesh,
        in_specs=(P("member", None, "gx", None), P(), P("gx"), P(), P("gx"), P("gx")),
        out_specs=P("member", None, "gx", None),
        check_vma=False,
    )
```

```python
import jax
import jax.numpy as jnp
from jax import lax
from jax.experimental import pallas as pl
from jax.experimental.pallas import tpu as pltpu
from jax.sharding import PartitionSpec as P

NS_ITERS = 6
COURANT = 0.6
DIFFUSE = 0.1
NS_PAIRS = 8
EARLY = 1
F32 = jnp.float32
BF16 = jnp.bfloat16
MESH = pl.DeviceIdType.MESH


def split2(x):
    hi = x.astype(BF16)
    lo = (x - hi.astype(F32)).astype(BF16)
    return hi, lo


def matmul(a, b):
    return lax.dot_general(a, b, (((1,), (0,)), ((), ())), preferred_element_type=F32)


def matmul_t(a, b):
    return lax.dot_general(a, b, (((1,), (1,)), ((), ())), preferred_element_type=F32)


def advance(west, center, east):
    shape = center.shape
    rows = center.reshape(-1, shape[-1])
    lane = lax.broadcasted_iota(jnp.int32, rows.shape, 1)
    south = jnp.where(lane == 0, 0.0, pltpu.roll(rows, 1, 1)).reshape(shape)
    north = jnp.where(lane == 127, 0.0, pltpu.roll(rows, 127, 1)).reshape(shape)
    return (
        center
        + COURANT * (west - center)
        + DIFFUSE * (west + east + south + north - 4.0 * center)
    )


def kernel(
    bg_hbm,
    col_hbm,
    radius_hbm,
    height_hbm,
    value_hbm,
    var_hbm,
    back_in,
    bg,
    col,
    radius,
    height,
    value,
    var,
    state,
    mid,
    fore,
    gathered,
    turned,
    weights,
    wgt,
    spread_ref,
    side,
    side_in,
    picked,
    picked_in,
    stage,
    back,
    load_sem,
    halo_send,
    halo_recv,
    side_send,
    side_recv,
    pick_send,
    pick_recv,
    fore_send,
    fore_recv,
    back_send,
    back_recv,
    keep_sem,
):
    me = lax.axis_index("member")
    tile = lax.axis_index("gx")
    group = 16
    tiles = lax.axis_size("gx")
    right = lax.rem(tile + 1, tiles)
    left = lax.rem(tile + tiles - 1, tiles)

    def load(i):
        pairs = (
            (bg_hbm, bg),
            (value_hbm, value),
            (var_hbm, var),
            (col_hbm, col),
            (height_hbm, height),
            (radius_hbm, radius),
        )
        return pltpu.make_async_copy(*pairs[i], load_sem.at[i])

    for i in range(6):
        load(i).start()

    barrier = pltpu.get_barrier_semaphore()

    def over_three(action):
        def body(d, carry):
            peer = lax.rem(me + d, group)
            action(0, d, {"member": peer, "gx": right})
            action(2, d, {"member": peer, "gx": left})

            @pl.when(d > 0)
            def _():
                action(1, d, {"member": peer})

            return carry

        lax.fori_loop(0, group, body, 0)

    over_three(
        lambda rel, d, device: pl.semaphore_signal(
            barrier, inc=1, device_id=device, device_id_type=MESH
        )
    )
    for i in range(6):
        load(i).wait()

    def rearrange(x, carry):
        for k in range(4):
            rows = bg[pl.ds(k * 256 + x, 16, stride=16), :]
            for fh in range(4):
                state[x + 2, fh, 4 * k : 4 * k + 4, :] = rows[4 * fh : 4 * fh + 4]
        return carry

    lax.fori_loop(0, 16, rearrange, 0)
    side[...] = jnp.concatenate(
        [
            jnp.concatenate([value[...], var[...]], axis=1),
            jnp.zeros((7, 128), F32),
        ],
        axis=0,
    )
    pl.semaphore_wait(barrier, 3 * group - 1)

    def halo(direction, part):
        which = pl.ds(0, 1) if part == 0 else pl.ds(1, 3)
        src, dst, peer = ((16, 0, right), (2, 18, left))[direction]
        slot = direction * 2 + part
        return pltpu.make_async_remote_copy(
            src_ref=state.at[pl.ds(src, 2), which],
            dst_ref=state.at[pl.ds(dst, 2), which],
            send_sem=halo_send.at[slot],
            recv_sem=halo_recv.at[slot],
            device_id={"gx": peer},
            device_id_type=MESH,
        )

    def to_side(direction):
        return pltpu.make_async_remote_copy(
            src_ref=side,
            dst_ref=side_in.at[direction],
            send_sem=side_send.at[direction],
            recv_sem=side_recv.at[direction],
            device_id={"gx": (right, left)[direction]},
            device_id_type=MESH,
        )

    for direction in range(2):
        halo(direction, 0).start()
    for direction in range(2):
        to_side(direction).start()
    for direction in range(2):
        halo(direction, 1).start()

    def first_step(index, which):
        mid[index, which] = advance(
            state[index, which], state[index + 1, which], state[index + 2, which]
        )

    def second_step(x, which):
        fore[x, which] = advance(mid[x, which], mid[x + 1, which], mid[x + 2, which])

    whole = pl.ds(0, 4)

    def inner_first(i, carry):
        for j in range(7):
            first_step(2 + 7 * i + j, whole)
        return carry

    def inner_second(i, carry):
        for j in range(6):
            second_step(2 + 6 * i + j, whole)
        return carry

    lax.fori_loop(0, 2, inner_first, 0)
    lax.fori_loop(0, 2, inner_second, 0)

    def send_fore(fh, peer):
        return pltpu.make_async_remote_copy(
            src_ref=fore.at[peer, fh],
            dst_ref=gathered.at[fh, pl.ds(pl.multiple_of(me * 16, 16), 16), :],
            send_sem=fore_send.at[fh],
            recv_sem=fore_recv.at[fh],
            device_id={"member": peer},
            device_id_type=MESH,
        )

    def over_peers(action):
        def body(d, carry):
            action(lax.rem(me + d, group))
            return carry

        lax.fori_loop(1, group, body, 0)

    def start_fore(groups, inner):
        def body(peer):
            is_inner = (peer >= 2) & (peer < 14)

            @pl.when(is_inner if inner else jnp.logical_not(is_inner))
            def _():
                for fh in groups:
                    send_fore(fh, peer).start()

        over_peers(body)

    early, late = range(EARLY), range(EARLY, 4)
    if EARLY:
        start_fore(early, True)

    def outer_rows(part):
        which = pl.ds(0, 1) if part == 0 else pl.ds(1, 3)
        count = 1 if part == 0 else 3
        for direction in range(2):
            halo(direction, part).wait_recv()
        nothing = jnp.zeros((count, 16, 128), F32)

        @pl.when(tile == 0)
        def _():
            state[0, which] = nothing
            state[1, which] = nothing

        @pl.when(tile == tiles - 1)
        def _():
            state[18, which] = nothing
            state[19, which] = nothing

        for index in (0, 1, 16, 17):
            first_step(index, which)

        @pl.when(tile == 0)
        def _():
            mid[0, which] = nothing

        @pl.when(tile == tiles - 1)
        def _():
            mid[17, which] = nothing

        for x in (0, 1, 14, 15):
            second_step(x, which)

    outer_rows(0)

    def tile_row(ref, t):
        row = ref[pl.ds(t // 2, 1), :]
        return jnp.where(lax.rem(t, 2) == 0, row[:, :64], row[:, 64:])

    own_col = tile_row(col, tile)
    own_x = own_col // 128 - tile * 16
    own_y = lax.rem(own_col, 128)
    hot_y = (lax.broadcasted_iota(jnp.int32, (128, 64), 0) == own_y).astype(F32).astype(BF16)
    observed = fore[:, 0].reshape(256, 128)
    hi, lo = split2(observed)
    low = (observed - hi.astype(F32) - lo.astype(F32)).astype(BF16)
    along_y = (matmul(hi, hot_y) + matmul(lo, hot_y)) + matmul(low, hot_y)
    total = jnp.zeros((16, 64), F32)
    for x in range(16):
        total = total + jnp.where(own_x == x, along_y[16 * x : 16 * x + 16], 0.0)
    level = lax.rem(lax.broadcasted_iota(jnp.int32, (16, 64), 0), 4)
    total = jnp.where(level == height[...], total, 0.0)
    sums = [jnp.sum(total[4 * k : 4 * k + 4], axis=0, keepdims=True) for k in range(4)]
    picked[...] = jnp.concatenate(
        [
            jnp.concatenate([sums[0], sums[1]], axis=1),
            jnp.concatenate([sums[2], sums[3]], axis=1),
        ],
        axis=0,
    )

    def send_picked(rel, d, device):
        return pltpu.make_async_remote_copy(
            src_ref=picked,
            dst_ref=picked_in.at[rel, me],
            send_sem=pick_send.at[rel, d],
            recv_sem=pick_recv.at[rel],
            device_id=device,
            device_id_type=MESH,
        )

    over_three(lambda rel, d, device: send_picked(rel, d, device).start())
    picked_in[1, me] = picked[...]
    if EARLY:
        start_fore(range(1), False)
    start_fore(late, True)

    outer_rows(1)
    start_fore(range(min(EARLY, 1), 4), False)
    gathered[:, pl.ds(pl.multiple_of(me * 16, 16), 16), :] = fore[me]

    def three(a, b, c, fill):
        return jnp.concatenate([a, b, c, jnp.full((1, 64), fill, a.dtype)], axis=1)

    before = jnp.maximum(tile - 1, 0)
    after = jnp.minimum(tile + 1, tiles - 1)
    near_col = three(tile_row(col, before), own_col, tile_row(col, after), 0)
    near_radius = three(
        tile_row(radius, before), tile_row(radius, tile), tile_row(radius, after), 1
    ).astype(F32)
    for direction in range(2):
        to_side(direction).wait_recv()
    from_left, own, from_right = side_in[0, 0:1, :], side[0:1, :], side_in[1, 0:1, :]
    near_value = three(from_left[:, :64], own[:, :64], from_right[:, :64], 0.0)
    near_var = three(from_left[:, 64:], own[:, 64:], from_right[:, 64:], 1.0)
    lane = lax.broadcasted_iota(jnp.int32, (1, 256), 1)
    first = jnp.where(tile == 0, 64, 0)
    last = jnp.where(tile == tiles - 1, 128, 192)
    valid = (lane >= first) & (lane < last)
    inverse = jnp.where(valid, 1.0 / near_var, 0.0)
    gap_along = (tile * 16 + me - near_col // 128).astype(F32)
    site = 4 * lax.broadcasted_iota(jnp.int32, (32, 256), 0)
    gap_across = (site - lax.rem(near_col, 128)).astype(F32)
    taper = jnp.maximum(
        0.0,
        1.0 - (gap_along * gap_along + gap_across * gap_across) / (near_radius * near_radius),
    )
    wgt[...] = taper * inverse

    def arrived(rel):
        count = 15 if rel == 1 else 16
        pltpu.make_async_copy(
            picked_in.at[rel, pl.ds(0, count)],
            picked_in.at[rel, pl.ds(0, count)],
            pick_recv.at[rel],
        ).wait()

    def by_member(rel):
        rows = jnp.concatenate([picked_in[rel, m] for m in range(16)], axis=0)
        return jnp.concatenate([rows[:, :64], rows[:, 64:]], axis=0)

    for rel in range(3):
        arrived(rel)
    ensemble = jnp.concatenate(
        [by_member(rel) for rel in range(3)] + [jnp.zeros((64, 64), F32)], axis=1
    )
    mean = jnp.sum(ensemble, axis=0, keepdims=True) / 64.0
    spread = ensemble - mean
    innovation = near_value - mean
    spread_ref[...] = spread
    spread_hi, spread_lo = split2(spread)
    across_obs = jnp.concatenate([spread_hi, spread_hi, spread_lo, spread_lo], axis=0)

    lane2 = lax.broadcasted_iota(jnp.int32, (64, 128), 1)
    row2 = lax.broadcasted_iota(jnp.int32, (64, 128), 0)
    is_first = lane2 < 64
    eye = (lax.rem(lane2, 64) == row2).astype(F32)
    is_first_row = lax.broadcasted_iota(jnp.int32, (1, 128), 1) < 64

    def operand(x):
        hi, lo = split2(x)
        return jnp.concatenate([hi, lo], axis=1)

    def stationary(x):
        hi = x.astype(BF16).astype(F32)
        lo = x - hi
        zero = jnp.zeros_like(x)
        top = jnp.concatenate(
            [jnp.where(is_first, hi, zero), jnp.where(is_first, lo, zero)], axis=1
        ).astype(BF16)
        bottom = jnp.concatenate(
            [jnp.where(is_first, zero, hi), jnp.where(is_first, zero, lo)], axis=1
        ).astype(BF16)
        return jnp.concatenate([top, bottom, top, bottom], axis=0)

    def fold(x):
        return x[:, :128] + x[:, 128:]

    def solve(batch):
        pairs = [batch * NS_PAIRS + i for i in range(NS_PAIRS)]
        system, drive = [], []
        for p in pairs:
            scaled = [spread_ref[...] * wgt[pl.ds(2 * p + h, 1), :] for h in range(2)]
            both = jnp.concatenate(scaled, axis=0)
            hi, lo = split2(both)
            product = fold(matmul_t(hi, across_obs)) + matmul_t(lo, across_obs[:128])
            system.append(jnp.where(is_first, product[:64], product[64:]) + 63.0 * eye)
            sums = [jnp.sum(s * innovation, axis=1, keepdims=True) for s in scaled]
            drive.append(jnp.where(is_first, sums[0], sums[1]))
        inv_norm, power, root = [], [], []
        for s in system:
            squares = jnp.sum(s * s, axis=0, keepdims=True)
            one = jnp.sum(jnp.where(is_first_row, squares, 0.0), axis=1, keepdims=True)
            two = jnp.sum(jnp.where(is_first_row, 0.0, squares), axis=1, keepdims=True)
            inv = 1.0 / jnp.sqrt(jnp.where(is_first_row, one, two))
            inv_norm.append(inv)
            power.append(s * inv)
        root = [1.5 * eye - 0.5 * p for p in power]
        for sweep in range(NS_ITERS - 1):
            fixed = [stationary(p) for p in power]
            moving = [operand(p) for p in power]
            if sweep == 0:
                square = [fold(matmul(m, f)) for m, f in zip(moving, fixed)]
            else:
                stacked = [
                    fold(matmul(jnp.concatenate([m, operand(z)], axis=0), f))
                    for m, z, f in zip(moving, root, fixed)
                ]
                square = [s[:64] for s in stacked]
                root = [1.5 * z - 0.5 * s[64:] for z, s in zip(root, stacked)]
            cube = [fold(matmul(operand(s), f)) for s, f in zip(square, fixed)]
            power = [2.25 * p - 1.5 * s + 0.25 * c for p, s, c in zip(power, square, cube)]
        root = [
            1.5 * z - 0.5 * fold(matmul(operand(z), stationary(p))) for z, p in zip(root, power)
        ]
        for p, z, inv, d in zip(pairs, root, inv_norm, drive):
            through = jnp.sum(z * d, axis=0, keepdims=True)
            again = z * through
            one = jnp.sum(jnp.where(is_first, again, 0.0), axis=1, keepdims=True)
            two = jnp.sum(jnp.where(is_first, 0.0, again), axis=1, keepdims=True)
            w = jnp.sqrt(63.0 * inv) * z + jnp.where(is_first, one, two) * inv
            w = w + (1.0 - jnp.sum(w, axis=0, keepdims=True)) * (1.0 / 64.0)
            hi = w.astype(BF16).astype(F32)
            lo = w - hi
            weights[2 * p] = jnp.where(is_first, hi, pltpu.roll(lo, 64, 1)).astype(BF16)
            weights[2 * p + 1] = jnp.where(is_first, pltpu.roll(hi, 64, 1), lo).astype(BF16)

    y8 = lax.broadcasted_iota(jnp.int32, (1, 8, 128), 1).astype(F32) * 0.25
    half = lax.broadcasted_iota(jnp.int32, (1, 8, 128), 2) < 64
    tent = [jnp.maximum(0.0, 1.0 - jnp.abs(y8 - c)) for c in range(3)]
    coef_a = jnp.where(half, tent[0], tent[1])
    coef_b = jnp.where(half, tent[2], 0.0)

    def all_bytes(buffer, sem):
        rows = buffer.at[pl.ds(0, buffer.shape[0] // group * (group - 1))]
        return pltpu.make_async_copy(rows, rows, sem)

    def send_back(half, peer):
        return pltpu.make_async_remote_copy(
            src_ref=back.at[half, pl.ds(pl.multiple_of(peer * 32, 32), 32), :],
            dst_ref=back_in.at[half, pl.ds(pl.multiple_of(me * 32, 32), 32), :],
            send_sem=back_send.at[half],
            recv_sem=back_recv.at[half],
            device_id={"member": peer},
            device_id_type=MESH,
        )

    def keep(half):
        rows = pl.ds(pl.multiple_of(me * 32, 32), 32)
        return pltpu.make_async_copy(
            back.at[half, rows], back_in.at[half, rows], keep_sem.at[half]
        )

    def turn(fh):
        for fl in range(4):
            rows = jnp.concatenate(
                [gathered[fh, pl.ds(fl + 4 * odd, 32, stride=8), :] for odd in range(2)], axis=0
            )
            turned[fh * 4 + fl] = jnp.concatenate([rows, rows], axis=0).T

    def blend(half, part):
        block = half * 8 + part
        rows = turned[:, pl.ds(pl.multiple_of(block * 8, 8), 8), :]
        near = operand((rows * coef_a).reshape(128, 128))
        far = operand((rows * coef_b).reshape(128, 128))
        c01 = weights[pl.ds(2 * block, 2)].reshape(128, 128)
        c23 = weights[pl.ds(2 * block + 2, 2)].reshape(128, 128)
        product = matmul(near, jnp.concatenate([c01, c01], axis=0)) + matmul(
            far, jnp.concatenate([c23, c23], axis=0)
        )
        product = (product[:, :64] + product[:, 64:]).reshape(8, 2, 8, 64)
        for odd in range(2):
            stage[:, 64 * odd + 8 * part : 64 * odd + 8 * part + 8, :] = product[:, odd]

    def half_step(step, carry):
        half = 1 - step
        solve(half)

        @pl.when(step == 0)
        def _():
            weights[32] = weights[31]
            weights[33] = jnp.zeros((64, 128), BF16)
            for fh in range(4):
                all_bytes(gathered.at[fh], fore_recv.at[fh]).wait()
                turn(fh)

        for part in range(8):
            blend(half, part)
        for pair in range(8):
            rows = stage[pair].T
            for odd in range(2):
                back[half, pl.ds(pair + 8 * odd, 32, stride=16), :] = rows[
                    32 * odd : 32 * odd + 32
                ]
        over_peers(lambda peer: send_back(half, peer).start())
        keep(half).start()
        return carry

    lax.fori_loop(0, 2, half_step, 0)

    for part in range(2):
        for direction in range(2):
            halo(direction, part).wait_send()
    for direction in range(2):
        to_side(direction).wait_send()
    over_three(lambda rel, d, device: send_picked(rel, d, device).wait_send())
    for fh in range(4):
        all_bytes(gathered.at[fh], fore_send.at[fh]).wait()
    for half in range(2):
        all_bytes(back.at[half], back_send.at[half]).wait()
        keep(half).wait()
    for half in range(2):
        all_bytes(back.at[half], back_recv.at[half]).wait()


def place(back_in, out, landed, placed, load_sem, leave_sem):
    lane = lax.broadcasted_iota(jnp.int32, (16, 128), 1)

    def load(half):
        return pltpu.make_async_copy(back_in.at[half], landed.at[half], load_sem.at[half])

    def leave(k):
        return pltpu.make_async_copy(placed.at[k], out.at[k], leave_sem.at[k])

    for half in range(2):
        load(half).start()
    for half in range(2):
        load(half).wait()
    for k in range(4):
        for pair in range(8):
            low, high = [
                landed[half, pl.ds(8 * k + pair, 16, stride=32), :] for half in range(2)
            ]
            placed[k, 2 * pair] = jnp.where(lane < 64, low, pltpu.roll(high, 64, 1))
            placed[k, 2 * pair + 1] = jnp.where(lane < 64, pltpu.roll(low, 64, 1), high)
        leave(k).start()
    for k in range(4):
        leave(k).wait()


def per_device(background_fields, obs_col, measured_height, obs_radius, obs_value, obs_var):
    dma = pltpu.SemaphoreType.DMA
    result = pl.pallas_call(
        kernel,
        out_shape=jax.ShapeDtypeStruct((2, 512, 128), F32),
        in_specs=[pl.BlockSpec(memory_space=pltpu.HBM)] * 6,
        out_specs=pl.BlockSpec(memory_space=pltpu.HBM),
        scratch_shapes=[
            pltpu.VMEM((1024, 128), F32),
            pltpu.VMEM((16, 128), jnp.int32),
            pltpu.VMEM((16, 128), jnp.int32),
            pltpu.VMEM((1, 64), jnp.int32),
            pltpu.VMEM((1, 64), F32),
            pltpu.VMEM((1, 64), F32),
            pltpu.VMEM((20, 4, 16, 128), F32),
            pltpu.VMEM((18, 4, 16, 128), F32),
            pltpu.VMEM((16, 4, 16, 128), F32),
            pltpu.VMEM((4, 256, 128), F32),
            pltpu.VMEM((16, 128, 128), F32),
            pltpu.VMEM((34, 64, 128), BF16),
            pltpu.VMEM((32, 256), F32),
            pltpu.VMEM((64, 256), F32),
            pltpu.VMEM((8, 128), F32),
            pltpu.VMEM((2, 8, 128), F32),
            pltpu.VMEM((2, 128), F32),
            pltpu.VMEM((3, 16, 2, 128), F32),
            pltpu.VMEM((8, 128, 64), F32),
            pltpu.VMEM((2, 512, 128), F32),
            dma((6,)),
            dma((4,)),
            dma((4,)),
            dma((2,)),
            dma((2,)),
            dma((3, 16)),
            dma((3,)),
            dma((4,)),
            dma((4,)),
            dma((2,)),
            dma((2,)),
            dma((2,)),
        ],
        compiler_params=pltpu.CompilerParams(
            collective_id=0, has_side_effects=True, vmem_limit_bytes=64 * 1024 * 1024
        ),
    )(
        *(
            pltpu.with_memory_space_constraint(x, pltpu.HBM)
            for x in (
                background_fields.reshape(1024, 128),
                obs_col.reshape(16, 128),
                obs_radius.reshape(16, 128),
                measured_height.reshape(1, 64),
                obs_value.reshape(1, 64),
                obs_var.reshape(1, 64),
            )
        )
    )
    return pl.pallas_call(
        place,
        out_shape=jax.ShapeDtypeStruct((4, 16, 16, 128), F32),
        in_specs=[pl.BlockSpec(memory_space=pltpu.HBM)],
        out_specs=pl.BlockSpec(memory_space=pltpu.HBM),
        scratch_shapes=[
            pltpu.VMEM((2, 512, 128), F32),
            pltpu.VMEM((4, 16, 16, 128), F32),
            dma((2,)),
            dma((4,)),
        ],
        compiler_params=pltpu.CompilerParams(vmem_limit_bytes=60 * 1024 * 1024),
    )(result)


def solution(mesh):
    return jax.shard_map(
        per_device,
        mesh=mesh,
        in_specs=(P("member", None, "gx", None), P(), P("gx"), P(), P("gx"), P("gx")),
        out_specs=P("member", None, "gx", None),
        check_vma=False,
    )
```

```python
import jax
import jax.numpy as jnp
from jax import lax
from jax.experimental import pallas as pl
from jax.experimental.pallas import tpu as pltpu
from jax.sharding import PartitionSpec as P

NS_ITERS = 6
COURANT = 0.6
DIFFUSE = 0.1
NS_PAIRS = 8
EARLY = 2
LATER_EARLY = 0
F32 = jnp.float32
BF16 = jnp.bfloat16
MESH = pl.DeviceIdType.MESH


def split2(x):
    hi = x.astype(BF16)
    lo = (x - hi.astype(F32)).astype(BF16)
    return hi, lo


def matmul(a, b):
    return lax.dot_general(a, b, (((1,), (0,)), ((), ())), preferred_element_type=F32)


def matmul_t(a, b):
    return lax.dot_general(a, b, (((1,), (1,)), ((), ())), preferred_element_type=F32)


def advance(west, center, east):
    shape = center.shape
    rows = center.reshape(-1, shape[-1])
    lane = lax.broadcasted_iota(jnp.int32, rows.shape, 1)
    south = jnp.where(lane == 0, 0.0, pltpu.roll(rows, 1, 1)).reshape(shape)
    north = jnp.where(lane == 127, 0.0, pltpu.roll(rows, 127, 1)).reshape(shape)
    return (
        center
        + COURANT * (west - center)
        + DIFFUSE * (west + east + south + north - 4.0 * center)
    )


def kernel(
    bg_hbm,
    col_hbm,
    radius_hbm,
    height_hbm,
    value_hbm,
    var_hbm,
    back_in,
    bg,
    col,
    radius,
    height,
    value,
    var,
    state,
    mid,
    low_fields,
    fore,
    gathered,
    turned,
    weights,
    wgt,
    spread_ref,
    side,
    side_in,
    picked,
    partial,
    beyond,
    edge,
    picked_in,
    beyond_in,
    stage,
    back,
    load_sem,
    halo_send,
    halo_recv,
    side_send,
    side_recv,
    pick_send,
    pick_recv,
    beyond_send,
    beyond_recv,
    ready,
    partner_ready,
    group_in,
    mate_in,
    fore_send,
    fore_recv,
    back_send,
    back_recv,
    keep_sem,
):
    me = lax.axis_index("member")
    tile = lax.axis_index("gx")
    group = 16
    tiles = lax.axis_size("gx")
    right = lax.rem(tile + 1, tiles)
    left = lax.rem(tile + tiles - 1, tiles)

    def load(i):
        pairs = (
            (bg_hbm, bg),
            (value_hbm, value),
            (var_hbm, var),
            (col_hbm, col),
            (height_hbm, height),
            (radius_hbm, radius),
        )
        return pltpu.make_async_copy(*pairs[i], load_sem.at[i])

    for i in range(6):
        load(i).start()

    core = lax.rem(tile, 2)
    later = lax.rem(tile // 2, 2) == 1
    mate = jnp.where(core == 0, right, left)
    across = jnp.where(core == 0, left, right)

    def signal(sem, device):
        pl.semaphore_signal(sem, inc=1, device_id=device, device_id_type=MESH)

    def over_group(action, start=0):
        def body(d, carry):
            action(lax.rem(me + d, group))
            return carry

        lax.fori_loop(start, group, body, 0)

    barrier = pltpu.get_barrier_semaphore()

    @pl.when(later)
    def _():
        signal(barrier, {"gx": mate})
        pl.semaphore_wait(barrier, group + 1)
        signal(partner_ready, {"gx": across})
        over_group(lambda peer: signal(ready, {"member": peer, "gx": across}), 1)

    @pl.when(jnp.logical_not(later))
    def _():
        over_group(lambda peer: signal(barrier, {"member": peer, "gx": across}))
        over_group(lambda peer: signal(barrier, {"member": peer}), 1)
        over_group(lambda peer: signal(barrier, {"member": peer, "gx": mate}))

    for i in range(6):
        load(i).wait()

    def rearrange(x, carry):
        for k in range(4):
            rows = bg[pl.ds(k * 256 + x, 16, stride=16), :]
            for fh in range(4):
                state[x + 2, fh, 4 * k : 4 * k + 4, :] = rows[4 * fh : 4 * fh + 4]
        return carry

    lax.fori_loop(0, 16, rearrange, 0)
    side[...] = jnp.concatenate(
        [
            jnp.concatenate([value[...], var[...]], axis=1),
            jnp.concatenate([height[...].astype(F32), jnp.zeros((1, 64), F32)], axis=1),
            jnp.zeros((6, 128), F32),
        ],
        axis=0,
    )

    @pl.when(jnp.logical_not(later))
    def _():
        pl.semaphore_wait(barrier, 2 * group - 1)

    def halo(direction, part):
        which = pl.ds(0, 1) if part == 0 else pl.ds(1, 3)
        src, dst, peer = ((16, 0, right), (2, 18, left))[direction]
        slot = direction * 2 + part
        return pltpu.make_async_remote_copy(
            src_ref=state.at[pl.ds(src, 2), which],
            dst_ref=state.at[pl.ds(dst, 2), which],
            send_sem=halo_send.at[slot],
            recv_sem=halo_recv.at[slot],
            device_id={"gx": peer},
            device_id_type=MESH,
        )

    def to_side(direction):
        return pltpu.make_async_remote_copy(
            src_ref=side,
            dst_ref=side_in.at[direction],
            send_sem=side_send.at[direction],
            recv_sem=side_recv.at[direction],
            device_id={"gx": (right, left)[direction]},
            device_id_type=MESH,
        )

    def to_mate():
        for direction in range(2):

            @pl.when(core == direction)
            def _():
                halo(direction, 0).start()
                to_side(direction).start()
                halo(direction, 1).start()

    def to_across():
        for direction in range(2):

            @pl.when(core != direction)
            def _():
                halo(direction, 0).start()
                to_side(direction).start()
                halo(direction, 1).start()

    @pl.when(later)
    def _():
        to_across()

    to_mate()

    def first_step(index, which):
        mid[index, which] = advance(
            state[index, which], state[index + 1, which], state[index + 2, which]
        )

    def second_step(x, which):
        return advance(mid[x, which], mid[x + 1, which], mid[x + 2, which])

    def pack(x, fields):
        is_left = lax.broadcasted_iota(jnp.int32, (16, 128), 1) < 64
        for fh in range(2):
            a, b = fields[fh], fields[fh + 2]
            fore[x, fh] = jnp.where(is_left, pltpu.roll(a, 64, 1), b)
            fore[x, 2 + fh] = jnp.where(is_left, a, pltpu.roll(b, 64, 1))


    def inner_rows(part):
        which = pl.ds(0, 1) if part == 0 else pl.ds(1, 3)

        def inner_first(i, carry):
            for j in range(7):
                first_step(2 + 7 * i + j, which)
            return carry

        def inner_second(i, carry):
            for j in range(6):
                x = 2 + 6 * i + j
                fields = second_step(x, which)
                if part == 0:
                    low_fields[x] = fields[0]
                else:
                    pack(x, [low_fields[x], fields[0], fields[1], fields[2]])
            return carry

        lax.fori_loop(0, 2, inner_first, 0)
        lax.fori_loop(0, 2, inner_second, 0)

    def send_fore(piece, peer):
        return pltpu.make_async_remote_copy(
            src_ref=fore.at[peer, piece],
            dst_ref=gathered.at[piece, pl.ds(pl.multiple_of(me * 16, 16), 16), :],
            send_sem=fore_send.at[piece],
            recv_sem=fore_recv.at[piece],
            device_id={"member": peer},
            device_id_type=MESH,
        )

    def over_peers(action):
        over_group(action, 1)

    def start_fore(inner_pieces, outer_pieces):
        def body(peer):
            is_inner = (peer >= 2) & (peer < 14)

            @pl.when(is_inner)
            def _():
                for piece in inner_pieces:
                    send_fore(piece, peer).start()

            @pl.when(jnp.logical_not(is_inner))
            def _():
                for piece in outer_pieces:
                    send_fore(piece, peer).start()

        over_peers(body)

    def edge_rows(part, direction):
        which = pl.ds(0, 1) if part == 0 else pl.ds(1, 3)
        count = 1 if part == 0 else 3
        halo(direction, part).wait_recv()
        nothing = jnp.zeros((count, 16, 128), F32)
        outside = tile == (0, tiles - 1)[direction]
        slots, firsts, seconds, beyond = (
            ((0, 1), (0, 1), (0, 1), 0),
            ((18, 19), (16, 17), (14, 15), 17),
        )[direction]

        @pl.when(outside)
        def _():
            for slot in slots:
                state[slot, which] = nothing

        for index in firsts:
            first_step(index, which)

        @pl.when(outside)
        def _():
            mid[beyond, which] = nothing

        for x in seconds:
            fields = second_step(x, which)
            if part == 0:
                low_fields[x] = fields[0]
            else:
                pack(x, [low_fields[x], fields[0], fields[1], fields[2]])

    def tile_row(ref, t):
        row = ref[pl.ds(t // 2, 1), :]
        return jnp.where(lax.rem(t, 2) == 0, row[:, :64], row[:, 64:])

    def hot(column):
        rows = lax.broadcasted_iota(jnp.int32, (128, 64), 0)
        return (rows == lax.rem(column, 128)).astype(F32).astype(BF16)

    def sample(rows, hot_y, along, levels):
        observed = jnp.concatenate(rows, axis=0)
        hi, lo = split2(observed)
        low = (observed - hi.astype(F32) - lo.astype(F32)).astype(BF16)
        along_y = (matmul(hi, hot_y) + matmul(lo, hot_y)) + matmul(low, hot_y)
        total = jnp.zeros((16, 64), F32)
        for i, x in enumerate(along[1]):
            total = total + jnp.where(along[0] == x, along_y[16 * i : 16 * i + 16], 0.0)
        level = lax.rem(lax.broadcasted_iota(jnp.int32, (16, 64), 0), 4)
        total = jnp.where(level == levels, total, 0.0)
        sums = [jnp.sum(total[4 * k : 4 * k + 4], axis=0, keepdims=True) for k in range(4)]
        return jnp.concatenate(
            [
                jnp.concatenate([sums[0], sums[1]], axis=1),
                jnp.concatenate([sums[2], sums[3]], axis=1),
            ],
            axis=0,
        )

    own_col = tile_row(col, tile)
    own_x = own_col // 128 - tile * 16
    hot_own = hot(own_col)

    def own_samples():
        rows = [low_fields[x] for x in range(16)]
        return sample(rows, hot_own, (own_x, range(16)), height[...])

    def send_picked(buffer, rel, device):
        return pltpu.make_async_remote_copy(
            src_ref=buffer,
            dst_ref=picked_in.at[rel, me],
            send_sem=pick_send.at[rel],
            recv_sem=pick_recv.at[rel],
            device_id=device,
            device_id_type=MESH,
        )

    def send_beyond(device):
        return pltpu.make_async_remote_copy(
            src_ref=beyond,
            dst_ref=beyond_in.at[me],
            send_sem=beyond_send,
            recv_sem=beyond_recv,
            device_id=device,
            device_id_type=MESH,
        )

    def over_tile(rel, action):
        def body(d, carry):
            peer = lax.rem(me + d, group)
            action({"member": peer} if rel == 1 else {"member": peer, "gx": (right, 0, left)[rel]})
            return carry

        lax.fori_loop(1 if rel == 1 else 0, group, body, 0)

    inner_rows(0)

    @pl.when(jnp.logical_not(later))
    def _():
        inner_rows(1)
        start_fore(range(EARLY), ())
        pl.semaphore_wait(partner_ready, 1)
        to_across()
        pl.semaphore_wait(ready, group - 1)
        signal(group_in, {"gx": across})

    none = jnp.zeros((16, 128), F32)

    @pl.when(core == 0)
    def _():
        edge_rows(0, 1)
        first, second = state[2, 0], state[3, 0]
        outer, inner = advance(none, none, first), advance(none, first, second)
        low_fields[0] = advance(outer, inner, mid[2, 0])
        low_fields[1] = advance(inner, mid[2, 0], mid[3, 0])
        edge[0] = advance(none, none, outer)
        edge[1] = advance(none, outer, inner)

    @pl.when(core == 1)
    def _():
        edge_rows(0, 0)
        first, second = state[17, 0], state[16, 0]
        outer, inner = advance(first, none, none), advance(second, first, none)
        low_fields[15] = advance(mid[15, 0], inner, outer)
        low_fields[14] = advance(mid[14, 0], mid[15, 0], inner)
        edge[0] = advance(inner, outer, none)
        edge[1] = advance(outer, none, none)

    @pl.when(later)
    def _():
        partial[...] = own_samples()

        @pl.when(core == 0)
        def _():
            over_tile(2, lambda device: send_picked(partial, 2, device).start())

        @pl.when(core == 1)
        def _():
            over_tile(0, lambda device: send_picked(partial, 0, device).start())

    @pl.when(later)
    def _():
        inner_rows(1)
        pl.semaphore_wait(group_in, 1)
        signal(mate_in, {"gx": mate})
        start_fore(range(LATER_EARLY), ())
        pl.semaphore_wait(mate_in, 1)

    @pl.when(core == 0)
    def _():
        edge_rows(0, 0)

    @pl.when(core == 1)
    def _():
        edge_rows(0, 1)

    for direction in range(2):
        to_side(direction).wait_recv()
    picked[...] = own_samples()
    over_tile(1, lambda device: send_picked(picked, 1, device).start())

    @pl.when(core == 0)
    def _():
        over_tile(0, lambda device: send_picked(picked, 0, device).start())

    @pl.when(core == 1)
    def _():
        over_tile(2, lambda device: send_picked(picked, 2, device).start())

    @pl.when(jnp.logical_not(later))
    def _():
        across_col = tile_row(col, across)
        across_x = across_col // 128 - across * 16 - jnp.where(core == 0, 14, 0)
        levels = jnp.where(core == 0, side_in[0, 1:2, :64], side_in[1, 1:2, :64])
        beyond[...] = sample(
            [edge[0], edge[1]],
            hot(across_col),
            (across_x, range(2)),
            levels.astype(jnp.int32),
        )
        beyond_in[me] = beyond[...]
        over_tile(1, lambda device: send_beyond(device).start())

        @pl.when(core == 0)
        def _():
            over_tile(2, lambda device: send_picked(picked, 2, device).start())

        @pl.when(core == 1)
        def _():
            over_tile(0, lambda device: send_picked(picked, 0, device).start())

    @pl.when(later)
    def _():
        beyond_in[...] = jnp.zeros((16, 2, 128), F32)

    picked_in[1, me] = picked[...]

    @pl.when(later)
    def _():
        start_fore(range(LATER_EARLY, 2), ())

    if EARLY < 2:

        @pl.when(jnp.logical_not(later))
        def _():
            start_fore(range(EARLY, 2), ())

    for direction in range(2):
        edge_rows(1, direction)
    start_fore((), range(2))

    @pl.when(later)
    def _():
        start_fore(range(2, 4), range(2, 4))

    @pl.when(jnp.logical_not(later))
    def _():
        start_fore(range(max(EARLY, 2), 4), range(2, 4))

    gathered[:, pl.ds(pl.multiple_of(me * 16, 16), 16), :] = fore[me]

    def three(a, b, c, fill):
        return jnp.concatenate([a, b, c, jnp.full((1, 64), fill, a.dtype)], axis=1)

    before = jnp.maximum(tile - 1, 0)
    after = jnp.minimum(tile + 1, tiles - 1)
    near_col = three(tile_row(col, before), own_col, tile_row(col, after), 0)
    near_radius = three(
        tile_row(radius, before), tile_row(radius, tile), tile_row(radius, after), 1
    ).astype(F32)
    from_left, own, from_right = side_in[0, 0:1, :], side[0:1, :], side_in[1, 0:1, :]
    near_value = three(from_left[:, :64], own[:, :64], from_right[:, :64], 0.0)
    near_var = three(from_left[:, 64:], own[:, 64:], from_right[:, 64:], 1.0)
    lane = lax.broadcasted_iota(jnp.int32, (1, 256), 1)
    first = jnp.where(tile == 0, 64, 0)
    last = jnp.where(tile == tiles - 1, 128, 192)
    valid = (lane >= first) & (lane < last)
    inverse = jnp.where(valid, 1.0 / near_var, 0.0)
    gap_along = (tile * 16 + me - near_col // 128).astype(F32)
    site = 4 * lax.broadcasted_iota(jnp.int32, (32, 256), 0)
    gap_across = (site - lax.rem(near_col, 128)).astype(F32)
    taper = jnp.maximum(
        0.0,
        1.0 - (gap_along * gap_along + gap_across * gap_across) / (near_radius * near_radius),
    )
    wgt[...] = taper * inverse

    def arrived(buffer, count, sem):
        rows = buffer.at[pl.ds(0, count)]
        pltpu.make_async_copy(rows, rows, sem).wait()

    def by_member(buffer):
        rows = jnp.concatenate([buffer[m] for m in range(16)], axis=0)
        return jnp.concatenate([rows[:, :64], rows[:, 64:]], axis=0)

    for rel in range(3):
        arrived(picked_in.at[rel], 15 if rel == 1 else 16, pick_recv.at[rel])

    @pl.when(jnp.logical_not(later))
    def _():
        arrived(beyond_in, 15, beyond_recv)

    added = by_member(beyond_in)
    ensemble = jnp.concatenate(
        [
            by_member(picked_in.at[0]) + jnp.where(core == 0, added, 0.0),
            by_member(picked_in.at[1]),
            by_member(picked_in.at[2]) + jnp.where(core == 1, added, 0.0),
            jnp.zeros((64, 64), F32),
        ],
        axis=1,
    )
    mean = jnp.sum(ensemble, axis=0, keepdims=True) / 64.0
    spread = ensemble - mean
    innovation = near_value - mean
    spread_ref[...] = spread
    spread_hi, spread_lo = split2(spread)
    across_obs = jnp.concatenate([spread_hi, spread_hi, spread_lo, spread_lo], axis=0)

    lane2 = lax.broadcasted_iota(jnp.int32, (64, 128), 1)
    row2 = lax.broadcasted_iota(jnp.int32, (64, 128), 0)
    is_first = lane2 < 64
    eye = (lax.rem(lane2, 64) == row2).astype(F32)
    is_first_row = lax.broadcasted_iota(jnp.int32, (1, 128), 1) < 64

    def operand(x):
        hi, lo = split2(x)
        return jnp.concatenate([hi, lo], axis=1)

    def stationary(x):
        hi = x.astype(BF16).astype(F32)
        lo = x - hi
        zero = jnp.zeros_like(x)
        top = jnp.concatenate(
            [jnp.where(is_first, hi, zero), jnp.where(is_first, lo, zero)], axis=1
        ).astype(BF16)
        bottom = jnp.concatenate(
            [jnp.where(is_first, zero, hi), jnp.where(is_first, zero, lo)], axis=1
        ).astype(BF16)
        return jnp.concatenate([top, bottom, top, bottom], axis=0)

    def fold(x):
        return x[:, :128] + x[:, 128:]

    def solve(batch):
        pairs = [batch * NS_PAIRS + i for i in range(NS_PAIRS)]
        system, drive = [], []
        for p in pairs:
            scaled = [spread_ref[...] * wgt[pl.ds(2 * p + h, 1), :] for h in range(2)]
            both = jnp.concatenate(scaled, axis=0)
            hi, lo = split2(both)
            product = fold(matmul_t(hi, across_obs)) + matmul_t(lo, across_obs[:128])
            system.append(jnp.where(is_first, product[:64], product[64:]) + 63.0 * eye)
            sums = [jnp.sum(s * innovation, axis=1, keepdims=True) for s in scaled]
            drive.append(jnp.where(is_first, sums[0], sums[1]))
        inv_norm, power, root = [], [], []
        for s in system:
            squares = jnp.sum(s * s, axis=0, keepdims=True)
            one = jnp.sum(jnp.where(is_first_row, squares, 0.0), axis=1, keepdims=True)
            two = jnp.sum(jnp.where(is_first_row, 0.0, squares), axis=1, keepdims=True)
            inv = 1.0 / jnp.sqrt(jnp.where(is_first_row, one, two))
            inv_norm.append(inv)
            power.append(s * inv)
        root = [1.5 * eye - 0.5 * p for p in power]
        for sweep in range(NS_ITERS - 1):
            fixed = [stationary(p) for p in power]
            moving = [operand(p) for p in power]
            if sweep == 0:
                square = [fold(matmul(m, f)) for m, f in zip(moving, fixed)]
            else:
                stacked = [
                    fold(matmul(jnp.concatenate([m, operand(z)], axis=0), f))
                    for m, z, f in zip(moving, root, fixed)
                ]
                square = [s[:64] for s in stacked]
                root = [1.5 * z - 0.5 * s[64:] for z, s in zip(root, stacked)]
            cube = [fold(matmul(operand(s), f)) for s, f in zip(square, fixed)]
            power = [2.25 * p - 1.5 * s + 0.25 * c for p, s, c in zip(power, square, cube)]
        root = [
            1.5 * z - 0.5 * fold(matmul(operand(z), stationary(p))) for z, p in zip(root, power)
        ]
        for p, z, inv, d in zip(pairs, root, inv_norm, drive):
            through = jnp.sum(z * d, axis=0, keepdims=True)
            again = z * through
            one = jnp.sum(jnp.where(is_first, again, 0.0), axis=1, keepdims=True)
            two = jnp.sum(jnp.where(is_first, 0.0, again), axis=1, keepdims=True)
            w = jnp.sqrt(63.0 * inv) * z + jnp.where(is_first, one, two) * inv
            w = w + (1.0 - jnp.sum(w, axis=0, keepdims=True)) * (1.0 / 64.0)
            hi = w.astype(BF16).astype(F32)
            lo = w - hi
            weights[2 * p] = jnp.where(is_first, hi, pltpu.roll(lo, 64, 1)).astype(BF16)
            weights[2 * p + 1] = jnp.where(is_first, pltpu.roll(hi, 64, 1), lo).astype(BF16)

    y8 = lax.broadcasted_iota(jnp.int32, (1, 8, 128), 1).astype(F32) * 0.25
    half = lax.broadcasted_iota(jnp.int32, (1, 8, 128), 2) < 64
    tent = [jnp.maximum(0.0, 1.0 - jnp.abs(y8 - c)) for c in range(3)]
    coef_a = jnp.where(half, tent[0], tent[1])
    coef_b = jnp.where(half, tent[2], 0.0)

    def all_bytes(buffer, sem):
        rows = buffer.at[pl.ds(0, buffer.shape[0] // group * (group - 1))]
        return pltpu.make_async_copy(rows, rows, sem)

    def send_back(half, peer):
        return pltpu.make_async_remote_copy(
            src_ref=back.at[half, pl.ds(pl.multiple_of(peer * 32, 32), 32), :],
            dst_ref=back_in.at[half, pl.ds(pl.multiple_of(me * 32, 32), 32), :],
            send_sem=back_send.at[half],
            recv_sem=back_recv.at[half],
            device_id={"member": peer},
            device_id_type=MESH,
        )

    def keep(half):
        rows = pl.ds(pl.multiple_of(me * 32, 32), 32)
        return pltpu.make_async_copy(
            back.at[half, rows], back_in.at[half, rows], keep_sem.at[half]
        )

    def turn(half, fh):
        piece = 2 * (1 - half) + fh
        all_bytes(gathered.at[piece], fore_recv.at[piece]).wait()
        for fl in range(4):
            rows = jnp.concatenate(
                [gathered[piece, pl.ds(fl + 4 * odd, 32, stride=8), :] for odd in range(2)], axis=0
            )
            columns = jnp.concatenate([rows, rows], axis=0).T
            turned[4 * fh + fl] = columns[:64]
            turned[8 + 4 * fh + fl] = columns[64:]

    def blend(half, part):
        block = half * 8 + part
        rows = turned[:, 8 * part : 8 * part + 8, :]
        near = operand((rows * coef_a).reshape(128, 128))
        far = operand((rows * coef_b).reshape(128, 128))
        c01 = weights[pl.ds(2 * block, 2)].reshape(128, 128)
        c23 = weights[pl.ds(2 * block + 2, 2)].reshape(128, 128)
        product = matmul(near, jnp.concatenate([c01, c01], axis=0)) + matmul(
            far, jnp.concatenate([c23, c23], axis=0)
        )
        product = (product[:, :64] + product[:, 64:]).reshape(8, 2, 8, 64)
        for odd in range(2):
            stage[:, 64 * odd + 8 * part : 64 * odd + 8 * part + 8, :] = product[:, odd]

    def half_step(step, carry):
        half = 1 - step
        solve(half)

        @pl.when(step == 0)
        def _():
            weights[32] = weights[31]
            weights[33] = jnp.zeros((64, 128), BF16)

        for fh in range(2):
            turn(half, fh)
        for part in range(8):
            blend(half, part)
        for pair in range(8):
            rows = stage[pair].T
            for odd in range(2):
                back[half, pl.ds(pair + 8 * odd, 32, stride=16), :] = rows[
                    32 * odd : 32 * odd + 32
                ]
        over_peers(lambda peer: send_back(half, peer).start())
        keep(half).start()
        return carry

    lax.fori_loop(0, 2, half_step, 0)

    for part in range(2):
        for direction in range(2):
            halo(direction, part).wait_send()
    for direction in range(2):
        to_side(direction).wait_send()
    for rel in range(3):
        arrived(picked_in.at[rel], 15 if rel == 1 else 16, pick_send.at[rel])

    @pl.when(jnp.logical_not(later))
    def _():
        arrived(beyond_in, 15, beyond_send)

    for fh in range(4):
        all_bytes(gathered.at[fh], fore_send.at[fh]).wait()
    for half in range(2):
        all_bytes(back.at[half], back_send.at[half]).wait()
        keep(half).wait()
    for half in range(2):
        all_bytes(back.at[half], back_recv.at[half]).wait()


def place(back_in, out, landed, placed, load_sem, leave_sem):
    lane = lax.broadcasted_iota(jnp.int32, (16, 128), 1)

    def load(half):
        return pltpu.make_async_copy(back_in.at[half], landed.at[half], load_sem.at[half])

    def leave(k):
        return pltpu.make_async_copy(placed.at[k], out.at[k], leave_sem.at[k])

    for half in range(2):
        load(half).start()
    for half in range(2):
        load(half).wait()
    for k in range(4):
        for pair in range(8):
            low, high = [
                landed[half, pl.ds(8 * k + pair, 16, stride=32), :] for half in range(2)
            ]
            placed[k, 2 * pair] = jnp.where(lane < 64, low, pltpu.roll(high, 64, 1))
            placed[k, 2 * pair + 1] = jnp.where(lane < 64, pltpu.roll(low, 64, 1), high)
        leave(k).start()
    for k in range(4):
        leave(k).wait()


def per_device(background_fields, obs_col, measured_height, obs_radius, obs_value, obs_var):
    dma = pltpu.SemaphoreType.DMA
    result = pl.pallas_call(
        kernel,
        out_shape=jax.ShapeDtypeStruct((2, 512, 128), F32),
        in_specs=[pl.BlockSpec(memory_space=pltpu.HBM)] * 6,
        out_specs=pl.BlockSpec(memory_space=pltpu.HBM),
        scratch_shapes=[
            pltpu.VMEM((1024, 128), F32),
            pltpu.VMEM((16, 128), jnp.int32),
            pltpu.VMEM((16, 128), jnp.int32),
            pltpu.VMEM((1, 64), jnp.int32),
            pltpu.VMEM((1, 64), F32),
            pltpu.VMEM((1, 64), F32),
            pltpu.VMEM((20, 4, 16, 128), F32),
            pltpu.VMEM((18, 4, 16, 128), F32),
            pltpu.VMEM((16, 16, 128), F32),
            pltpu.VMEM((16, 4, 16, 128), F32),
            pltpu.VMEM((4, 256, 128), F32),
            pltpu.VMEM((16, 64, 128), F32),
            pltpu.VMEM((34, 64, 128), BF16),
            pltpu.VMEM((32, 256), F32),
            pltpu.VMEM((64, 256), F32),
            pltpu.VMEM((8, 128), F32),
            pltpu.VMEM((2, 8, 128), F32),
            pltpu.VMEM((2, 128), F32),
            pltpu.VMEM((2, 128), F32),
            pltpu.VMEM((2, 128), F32),
            pltpu.VMEM((2, 16, 128), F32),
            pltpu.VMEM((3, 16, 2, 128), F32),
            pltpu.VMEM((16, 2, 128), F32),
            pltpu.VMEM((8, 128, 64), F32),
            pltpu.VMEM((2, 512, 128), F32),
            dma((6,)),
            dma((4,)),
            dma((4,)),
            dma((2,)),
            dma((2,)),
            dma((3,)),
            dma((3,)),
            dma,
            dma,
            pltpu.SemaphoreType.REGULAR,
            pltpu.SemaphoreType.REGULAR,
            pltpu.SemaphoreType.REGULAR,
            pltpu.SemaphoreType.REGULAR,
            dma((4,)),
            dma((4,)),
            dma((2,)),
            dma((2,)),
            dma((2,)),
        ],
        compiler_params=pltpu.CompilerParams(
            collective_id=0, has_side_effects=True, vmem_limit_bytes=64 * 1024 * 1024
        ),
    )(
        *(
            pltpu.with_memory_space_constraint(x, pltpu.HBM)
            for x in (
                background_fields.reshape(1024, 128),
                obs_col.reshape(16, 128),
                obs_radius.reshape(16, 128),
                measured_height.reshape(1, 64),
                obs_value.reshape(1, 64),
                obs_var.reshape(1, 64),
            )
        )
    )
    return pl.pallas_call(
        place,
        out_shape=jax.ShapeDtypeStruct((4, 16, 16, 128), F32),
        in_specs=[pl.BlockSpec(memory_space=pltpu.HBM)],
        out_specs=pl.BlockSpec(memory_space=pltpu.HBM),
        scratch_shapes=[
            pltpu.VMEM((2, 512, 128), F32),
            pltpu.VMEM((4, 16, 16, 128), F32),
            dma((2,)),
            dma((4,)),
        ],
        compiler_params=pltpu.CompilerParams(vmem_limit_bytes=60 * 1024 * 1024),
    )(result)


def solution(mesh):
    return jax.shard_map(
        per_device,
        mesh=mesh,
        in_specs=(P("member", None, "gx", None), P(), P("gx"), P(), P("gx"), P("gx")),
        out_specs=P("member", None, "gx", None),
        check_vma=False,
    )
```

```python
import jax
import jax.numpy as jnp
from jax import lax
from jax.experimental import pallas as pl
from jax.experimental.pallas import tpu as pltpu
from jax.sharding import PartitionSpec as P

NS_ITERS = 6
COURANT = 0.6
DIFFUSE = 0.1
NS_PAIRS = 8
EARLY = 2
LATER_EARLY = 1
F32 = jnp.float32
BF16 = jnp.bfloat16
MESH = pl.DeviceIdType.MESH


def split2(x):
    hi = x.astype(BF16)
    lo = (x - hi.astype(F32)).astype(BF16)
    return hi, lo


def matmul(a, b):
    return lax.dot_general(a, b, (((1,), (0,)), ((), ())), preferred_element_type=F32)


def matmul_t(a, b):
    return lax.dot_general(a, b, (((1,), (1,)), ((), ())), preferred_element_type=F32)


def advance(west, center, east):
    shape = center.shape
    rows = center.reshape(-1, shape[-1])
    lane = lax.broadcasted_iota(jnp.int32, rows.shape, 1)
    south = jnp.where(lane == 0, 0.0, pltpu.roll(rows, 1, 1)).reshape(shape)
    north = jnp.where(lane == 127, 0.0, pltpu.roll(rows, 127, 1)).reshape(shape)
    return (
        center
        + COURANT * (west - center)
        + DIFFUSE * (west + east + south + north - 4.0 * center)
    )


def kernel(
    bg_hbm,
    col_hbm,
    radius_hbm,
    height_hbm,
    value_hbm,
    var_hbm,
    back_in,
    bg,
    col,
    radius,
    height,
    value,
    var,
    state,
    mid,
    low_fields,
    fore,
    gathered,
    turned,
    weights,
    wgt,
    spread_ref,
    side,
    side_in,
    picked,
    partial,
    beyond,
    edge,
    picked_in,
    beyond_in,
    stage,
    back,
    load_sem,
    halo_send,
    halo_recv,
    side_send,
    side_recv,
    pick_send,
    pick_recv,
    beyond_send,
    beyond_recv,
    ready,
    partner_ready,
    group_in,
    mate_in,
    fore_send,
    fore_recv,
    back_send,
    back_recv,
    keep_sem,
):
    me = lax.axis_index("member")
    tile = lax.axis_index("gx")
    group = 16
    tiles = lax.axis_size("gx")
    right = lax.rem(tile + 1, tiles)
    left = lax.rem(tile + tiles - 1, tiles)

    def load(i):
        pairs = (
            (bg_hbm, bg),
            (value_hbm, value),
            (var_hbm, var),
            (col_hbm, col),
            (height_hbm, height),
            (radius_hbm, radius),
        )
        return pltpu.make_async_copy(*pairs[i], load_sem.at[i])

    for i in range(6):
        load(i).start()

    core = lax.rem(tile, 2)
    later = lax.rem(tile // 2, 2) == 1
    mate = jnp.where(core == 0, right, left)
    across = jnp.where(core == 0, left, right)

    def signal(sem, device):
        pl.semaphore_signal(sem, inc=1, device_id=device, device_id_type=MESH)

    def over_group(action, start=0):
        def body(d, carry):
            action(lax.rem(me + d, group))
            return carry

        lax.fori_loop(start, group, body, 0)

    barrier = pltpu.get_barrier_semaphore()

    @pl.when(later)
    def _():
        signal(barrier, {"gx": mate})
        pl.semaphore_wait(barrier, group + 1)
        signal(partner_ready, {"gx": across})
        over_group(lambda peer: signal(ready, {"member": peer, "gx": across}), 1)

    @pl.when(jnp.logical_not(later))
    def _():
        over_group(lambda peer: signal(barrier, {"member": peer, "gx": across}))
        over_group(lambda peer: signal(barrier, {"member": peer}), 1)
        over_group(lambda peer: signal(barrier, {"member": peer, "gx": mate}))

    for i in range(6):
        load(i).wait()

    def rearrange(x, carry):
        for k in range(4):
            rows = bg[pl.ds(k * 256 + x, 16, stride=16), :]
            for fh in range(4):
                state[x + 2, fh, 4 * k : 4 * k + 4, :] = rows[4 * fh : 4 * fh + 4]
        return carry

    lax.fori_loop(0, 16, rearrange, 0)
    side[...] = jnp.concatenate(
        [
            jnp.concatenate([value[...], var[...]], axis=1),
            jnp.concatenate([height[...].astype(F32), jnp.zeros((1, 64), F32)], axis=1),
            jnp.zeros((6, 128), F32),
        ],
        axis=0,
    )

    @pl.when(jnp.logical_not(later))
    def _():
        pl.semaphore_wait(barrier, 2 * group - 1)

    def halo(direction, part):
        which = pl.ds(0, 1) if part == 0 else pl.ds(1, 3)
        src, dst, peer = ((16, 0, right), (2, 18, left))[direction]
        slot = direction * 2 + part
        return pltpu.make_async_remote_copy(
            src_ref=state.at[pl.ds(src, 2), which],
            dst_ref=state.at[pl.ds(dst, 2), which],
            send_sem=halo_send.at[slot],
            recv_sem=halo_recv.at[slot],
            device_id={"gx": peer},
            device_id_type=MESH,
        )

    def to_side(direction):
        return pltpu.make_async_remote_copy(
            src_ref=side,
            dst_ref=side_in.at[direction],
            send_sem=side_send.at[direction],
            recv_sem=side_recv.at[direction],
            device_id={"gx": (right, left)[direction]},
            device_id_type=MESH,
        )

    def to_mate():
        for direction in range(2):

            @pl.when(core == direction)
            def _():
                halo(direction, 0).start()
                to_side(direction).start()
                halo(direction, 1).start()

    def to_across():
        for direction in range(2):

            @pl.when(core != direction)
            def _():
                halo(direction, 0).start()
                to_side(direction).start()
                halo(direction, 1).start()

    @pl.when(later)
    def _():
        to_across()

    to_mate()

    def first_step(index, which):
        mid[index, which] = advance(
            state[index, which], state[index + 1, which], state[index + 2, which]
        )

    def second_step(x, which):
        return advance(mid[x, which], mid[x + 1, which], mid[x + 2, which])

    def pack(x, fields):
        is_left = lax.broadcasted_iota(jnp.int32, (16, 128), 1) < 64
        for fh in range(2):
            a, b = fields[fh], fields[fh + 2]
            fore[x, fh] = jnp.where(is_left, pltpu.roll(a, 64, 1), b)
            fore[x, 2 + fh] = jnp.where(is_left, a, pltpu.roll(b, 64, 1))


    def inner_rows(part):
        which = pl.ds(0, 1) if part == 0 else pl.ds(1, 3)

        def inner_first(i, carry):
            for j in range(7):
                first_step(2 + 7 * i + j, which)
            return carry

        def inner_second(i, carry):
            for j in range(6):
                x = 2 + 6 * i + j
                fields = second_step(x, which)
                if part == 0:
                    low_fields[x] = fields[0]
                else:
                    pack(x, [low_fields[x], fields[0], fields[1], fields[2]])
            return carry

        lax.fori_loop(0, 2, inner_first, 0)
        lax.fori_loop(0, 2, inner_second, 0)

    def send_fore(piece, peer):
        return pltpu.make_async_remote_copy(
            src_ref=fore.at[peer, piece],
            dst_ref=gathered.at[piece, pl.ds(pl.multiple_of(me * 16, 16), 16), :],
            send_sem=fore_send.at[piece],
            recv_sem=fore_recv.at[piece],
            device_id={"member": peer},
            device_id_type=MESH,
        )

    def over_peers(action):
        over_group(action, 1)

    def start_fore(inner_pieces, outer_pieces):
        def body(peer):
            is_inner = (peer >= 2) & (peer < 14)

            @pl.when(is_inner)
            def _():
                for piece in inner_pieces:
                    send_fore(piece, peer).start()

            @pl.when(jnp.logical_not(is_inner))
            def _():
                for piece in outer_pieces:
                    send_fore(piece, peer).start()

        over_peers(body)

    def edge_rows(part, direction):
        which = pl.ds(0, 1) if part == 0 else pl.ds(1, 3)
        count = 1 if part == 0 else 3
        halo(direction, part).wait_recv()
        nothing = jnp.zeros((count, 16, 128), F32)
        outside = tile == (0, tiles - 1)[direction]
        slots, firsts, seconds, beyond = (
            ((0, 1), (0, 1), (0, 1), 0),
            ((18, 19), (16, 17), (14, 15), 17),
        )[direction]

        @pl.when(outside)
        def _():
            for slot in slots:
                state[slot, which] = nothing

        for index in firsts:
            first_step(index, which)

        @pl.when(outside)
        def _():
            mid[beyond, which] = nothing

        for x in seconds:
            fields = second_step(x, which)
            if part == 0:
                low_fields[x] = fields[0]
            else:
                pack(x, [low_fields[x], fields[0], fields[1], fields[2]])

    def tile_row(ref, t):
        row = ref[pl.ds(t // 2, 1), :]
        return jnp.where(lax.rem(t, 2) == 0, row[:, :64], row[:, 64:])

    def hot(column):
        rows = lax.broadcasted_iota(jnp.int32, (128, 64), 0)
        return (rows == lax.rem(column, 128)).astype(F32).astype(BF16)

    def sample(rows, hot_y, along, levels):
        observed = jnp.concatenate(rows, axis=0)
        hi, lo = split2(observed)
        low = (observed - hi.astype(F32) - lo.astype(F32)).astype(BF16)
        along_y = (matmul(hi, hot_y) + matmul(lo, hot_y)) + matmul(low, hot_y)
        total = jnp.zeros((16, 64), F32)
        for i, x in enumerate(along[1]):
            total = total + jnp.where(along[0] == x, along_y[16 * i : 16 * i + 16], 0.0)
        level = lax.rem(lax.broadcasted_iota(jnp.int32, (16, 64), 0), 4)
        total = jnp.where(level == levels, total, 0.0)
        sums = [jnp.sum(total[4 * k : 4 * k + 4], axis=0, keepdims=True) for k in range(4)]
        return jnp.concatenate(
            [
                jnp.concatenate([sums[0], sums[1]], axis=1),
                jnp.concatenate([sums[2], sums[3]], axis=1),
            ],
            axis=0,
        )

    own_col = tile_row(col, tile)
    own_x = own_col // 128 - tile * 16
    hot_own = hot(own_col)

    def own_samples():
        rows = [low_fields[x] for x in range(16)]
        return sample(rows, hot_own, (own_x, range(16)), height[...])

    def send_picked(buffer, rel, device):
        return pltpu.make_async_remote_copy(
            src_ref=buffer,
            dst_ref=picked_in.at[rel, me],
            send_sem=pick_send.at[rel],
            recv_sem=pick_recv.at[rel],
            device_id=device,
            device_id_type=MESH,
        )

    def send_beyond(device):
        return pltpu.make_async_remote_copy(
            src_ref=beyond,
            dst_ref=beyond_in.at[me],
            send_sem=beyond_send,
            recv_sem=beyond_recv,
            device_id=device,
            device_id_type=MESH,
        )

    def over_tile(rel, action):
        def body(d, carry):
            peer = lax.rem(me + d, group)
            action({"member": peer} if rel == 1 else {"member": peer, "gx": (right, 0, left)[rel]})
            return carry

        lax.fori_loop(1 if rel == 1 else 0, group, body, 0)

    inner_rows(0)

    @pl.when(jnp.logical_not(later))
    def _():
        inner_rows(1)
        start_fore(range(EARLY), ())
        pl.semaphore_wait(partner_ready, 1)
        to_across()

    none = jnp.zeros((16, 128), F32)

    @pl.when(core == 0)
    def _():
        edge_rows(0, 1)
        first, second = state[2, 0], state[3, 0]
        outer, inner = advance(none, none, first), advance(none, first, second)
        low_fields[0] = advance(outer, inner, mid[2, 0])
        low_fields[1] = advance(inner, mid[2, 0], mid[3, 0])
        edge[0] = advance(none, none, outer)
        edge[1] = advance(none, outer, inner)

    @pl.when(core == 1)
    def _():
        edge_rows(0, 0)
        first, second = state[17, 0], state[16, 0]
        outer, inner = advance(first, none, none), advance(second, first, none)
        low_fields[15] = advance(mid[15, 0], inner, outer)
        low_fields[14] = advance(mid[14, 0], mid[15, 0], inner)
        edge[0] = advance(inner, outer, none)
        edge[1] = advance(outer, none, none)

    @pl.when(later)
    def _():
        partial[...] = own_samples()

        @pl.when(core == 0)
        def _():
            over_tile(2, lambda device: send_picked(partial, 2, device).start())

        @pl.when(core == 1)
        def _():
            over_tile(0, lambda device: send_picked(partial, 0, device).start())

    @pl.when(later)
    def _():
        inner_rows(1)
        pl.semaphore_wait(group_in, 1)
        signal(mate_in, {"gx": mate})
        start_fore(range(LATER_EARLY), ())
        pl.semaphore_wait(mate_in, 1)

    @pl.when(jnp.logical_not(later))
    def _():
        pl.semaphore_wait(ready, group - 1)
        signal(group_in, {"gx": across})

    @pl.when(core == 0)
    def _():
        edge_rows(0, 0)

    @pl.when(core == 1)
    def _():
        edge_rows(0, 1)

    for direction in range(2):
        to_side(direction).wait_recv()
    picked[...] = own_samples()
    over_tile(1, lambda device: send_picked(picked, 1, device).start())

    @pl.when(core == 0)
    def _():
        over_tile(0, lambda device: send_picked(picked, 0, device).start())

    @pl.when(core == 1)
    def _():
        over_tile(2, lambda device: send_picked(picked, 2, device).start())

    @pl.when(jnp.logical_not(later))
    def _():
        across_col = tile_row(col, across)
        across_x = across_col // 128 - across * 16 - jnp.where(core == 0, 14, 0)
        levels = jnp.where(core == 0, side_in[0, 1:2, :64], side_in[1, 1:2, :64])
        beyond[...] = sample(
            [edge[0], edge[1]],
            hot(across_col),
            (across_x, range(2)),
            levels.astype(jnp.int32),
        )
        beyond_in[me] = beyond[...]
        over_tile(1, lambda device: send_beyond(device).start())

        @pl.when(core == 0)
        def _():
            over_tile(2, lambda device: send_picked(picked, 2, device).start())

        @pl.when(core == 1)
        def _():
            over_tile(0, lambda device: send_picked(picked, 0, device).start())

    @pl.when(later)
    def _():
        beyond_in[...] = jnp.zeros((16, 2, 128), F32)

    picked_in[1, me] = picked[...]

    @pl.when(later)
    def _():
        start_fore(range(LATER_EARLY, 2), ())

    if EARLY < 2:

        @pl.when(jnp.logical_not(later))
        def _():
            start_fore(range(EARLY, 2), ())

    for direction in range(2):
        edge_rows(1, direction)
    start_fore((), range(2))

    @pl.when(later)
    def _():
        start_fore(range(2, 4), range(2, 4))

    @pl.when(jnp.logical_not(later))
    def _():
        start_fore(range(max(EARLY, 2), 4), range(2, 4))

    gathered[:, pl.ds(pl.multiple_of(me * 16, 16), 16), :] = fore[me]

    def three(a, b, c, fill):
        return jnp.concatenate([a, b, c, jnp.full((1, 64), fill, a.dtype)], axis=1)

    before = jnp.maximum(tile - 1, 0)
    after = jnp.minimum(tile + 1, tiles - 1)
    near_col = three(tile_row(col, before), own_col, tile_row(col, after), 0)
    near_radius = three(
        tile_row(radius, before), tile_row(radius, tile), tile_row(radius, after), 1
    ).astype(F32)
    from_left, own, from_right = side_in[0, 0:1, :], side[0:1, :], side_in[1, 0:1, :]
    near_value = three(from_left[:, :64], own[:, :64], from_right[:, :64], 0.0)
    near_var = three(from_left[:, 64:], own[:, 64:], from_right[:, 64:], 1.0)
    lane = lax.broadcasted_iota(jnp.int32, (1, 256), 1)
    first = jnp.where(tile == 0, 64, 0)
    last = jnp.where(tile == tiles - 1, 128, 192)
    valid = (lane >= first) & (lane < last)
    inverse = jnp.where(valid, 1.0 / near_var, 0.0)
    gap_along = (tile * 16 + me - near_col // 128).astype(F32)
    site = 4 * lax.broadcasted_iota(jnp.int32, (32, 256), 0)
    gap_across = (site - lax.rem(near_col, 128)).astype(F32)
    taper = jnp.maximum(
        0.0,
        1.0 - (gap_along * gap_along + gap_across * gap_across) / (near_radius * near_radius),
    )
    wgt[...] = taper * inverse

    def arrived(buffer, count, sem):
        rows = buffer.at[pl.ds(0, count)]
        pltpu.make_async_copy(rows, rows, sem).wait()

    def by_member(buffer):
        rows = jnp.concatenate([buffer[m] for m in range(16)], axis=0)
        return jnp.concatenate([rows[:, :64], rows[:, 64:]], axis=0)

    for rel in range(3):
        arrived(picked_in.at[rel], 15 if rel == 1 else 16, pick_recv.at[rel])

    @pl.when(jnp.logical_not(later))
    def _():
        arrived(beyond_in, 15, beyond_recv)

    added = by_member(beyond_in)
    ensemble = jnp.concatenate(
        [
            by_member(picked_in.at[0]) + jnp.where(core == 0, added, 0.0),
            by_member(picked_in.at[1]),
            by_member(picked_in.at[2]) + jnp.where(core == 1, added, 0.0),
            jnp.zeros((64, 64), F32),
        ],
        axis=1,
    )
    mean = jnp.sum(ensemble, axis=0, keepdims=True) / 64.0
    spread = ensemble - mean
    innovation = near_value - mean
    spread_ref[...] = spread
    spread_hi, spread_lo = split2(spread)
    across_obs = jnp.concatenate([spread_hi, spread_hi, spread_lo, spread_lo], axis=0)

    lane2 = lax.broadcasted_iota(jnp.int32, (64, 128), 1)
    row2 = lax.broadcasted_iota(jnp.int32, (64, 128), 0)
    is_first = lane2 < 64
    eye = (lax.rem(lane2, 64) == row2).astype(F32)
    is_first_row = lax.broadcasted_iota(jnp.int32, (1, 128), 1) < 64

    def operand(x):
        hi, lo = split2(x)
        return jnp.concatenate([hi, lo], axis=1)

    def stationary(x):
        hi = x.astype(BF16).astype(F32)
        lo = x - hi
        zero = jnp.zeros_like(x)
        top = jnp.concatenate(
            [jnp.where(is_first, hi, zero), jnp.where(is_first, lo, zero)], axis=1
        ).astype(BF16)
        bottom = jnp.concatenate(
            [jnp.where(is_first, zero, hi), jnp.where(is_first, zero, lo)], axis=1
        ).astype(BF16)
        return jnp.concatenate([top, bottom, top, bottom], axis=0)

    def fold(x):
        return x[:, :128] + x[:, 128:]

    def solve(batch):
        pairs = [batch * NS_PAIRS + i for i in range(NS_PAIRS)]
        system, drive = [], []
        for p in pairs:
            scaled = [spread_ref[...] * wgt[pl.ds(2 * p + h, 1), :] for h in range(2)]
            both = jnp.concatenate(scaled, axis=0)
            hi, lo = split2(both)
            product = fold(matmul_t(hi, across_obs)) + matmul_t(lo, across_obs[:128])
            system.append(jnp.where(is_first, product[:64], product[64:]) + 63.0 * eye)
            sums = [jnp.sum(s * innovation, axis=1, keepdims=True) for s in scaled]
            drive.append(jnp.where(is_first, sums[0], sums[1]))
        inv_norm, power, root = [], [], []
        for s in system:
            squares = jnp.sum(s * s, axis=0, keepdims=True)
            one = jnp.sum(jnp.where(is_first_row, squares, 0.0), axis=1, keepdims=True)
            two = jnp.sum(jnp.where(is_first_row, 0.0, squares), axis=1, keepdims=True)
            inv = 1.0 / jnp.sqrt(jnp.where(is_first_row, one, two))
            inv_norm.append(inv)
            power.append(s * inv)
        root = [1.5 * eye - 0.5 * p for p in power]
        for sweep in range(NS_ITERS - 1):
            fixed = [stationary(p) for p in power]
            moving = [operand(p) for p in power]
            if sweep == 0:
                square = [fold(matmul(m, f)) for m, f in zip(moving, fixed)]
            else:
                stacked = [
                    fold(matmul(jnp.concatenate([m, operand(z)], axis=0), f))
                    for m, z, f in zip(moving, root, fixed)
                ]
                square = [s[:64] for s in stacked]
                root = [1.5 * z - 0.5 * s[64:] for z, s in zip(root, stacked)]
            cube = [fold(matmul(operand(s), f)) for s, f in zip(square, fixed)]
            power = [2.25 * p - 1.5 * s + 0.25 * c for p, s, c in zip(power, square, cube)]
        root = [
            1.5 * z - 0.5 * fold(matmul(operand(z), stationary(p))) for z, p in zip(root, power)
        ]
        for p, z, inv, d in zip(pairs, root, inv_norm, drive):
            through = jnp.sum(z * d, axis=0, keepdims=True)
            again = z * through
            one = jnp.sum(jnp.where(is_first, again, 0.0), axis=1, keepdims=True)
            two = jnp.sum(jnp.where(is_first, 0.0, again), axis=1, keepdims=True)
            w = jnp.sqrt(63.0 * inv) * z + jnp.where(is_first, one, two) * inv
            w = w + (1.0 - jnp.sum(w, axis=0, keepdims=True)) * (1.0 / 64.0)
            hi = w.astype(BF16).astype(F32)
            lo = w - hi
            weights[2 * p] = jnp.where(is_first, hi, pltpu.roll(lo, 64, 1)).astype(BF16)
            weights[2 * p + 1] = jnp.where(is_first, pltpu.roll(hi, 64, 1), lo).astype(BF16)

    y8 = lax.broadcasted_iota(jnp.int32, (1, 8, 128), 1).astype(F32) * 0.25
    half = lax.broadcasted_iota(jnp.int32, (1, 8, 128), 2) < 64
    tent = [jnp.maximum(0.0, 1.0 - jnp.abs(y8 - c)) for c in range(3)]
    coef_a = jnp.where(half, tent[0], tent[1])
    coef_b = jnp.where(half, tent[2], 0.0)

    def all_bytes(buffer, sem):
        rows = buffer.at[pl.ds(0, buffer.shape[0] // group * (group - 1))]
        return pltpu.make_async_copy(rows, rows, sem)

    def send_back(half, peer):
        return pltpu.make_async_remote_copy(
            src_ref=back.at[half, pl.ds(pl.multiple_of(peer * 32, 32), 32), :],
            dst_ref=back_in.at[half, pl.ds(pl.multiple_of(me * 32, 32), 32), :],
            send_sem=back_send.at[half],
            recv_sem=back_recv.at[half],
            device_id={"member": peer},
            device_id_type=MESH,
        )

    def keep(half):
        rows = pl.ds(pl.multiple_of(me * 32, 32), 32)
        return pltpu.make_async_copy(
            back.at[half, rows], back_in.at[half, rows], keep_sem.at[half]
        )

    def turn(half, fh):
        piece = 2 * (1 - half) + fh
        all_bytes(gathered.at[piece], fore_recv.at[piece]).wait()
        for fl in range(4):
            rows = jnp.concatenate(
                [gathered[piece, pl.ds(fl + 4 * odd, 32, stride=8), :] for odd in range(2)], axis=0
            )
            columns = jnp.concatenate([rows, rows], axis=0).T
            turned[4 * fh + fl] = columns[:64]
            turned[8 + 4 * fh + fl] = columns[64:]

    def blend(half, part):
        block = half * 8 + part
        rows = turned[:, 8 * part : 8 * part + 8, :]
        near = operand((rows * coef_a).reshape(128, 128))
        far = operand((rows * coef_b).reshape(128, 128))
        c01 = weights[pl.ds(2 * block, 2)].reshape(128, 128)
        c23 = weights[pl.ds(2 * block + 2, 2)].reshape(128, 128)
        product = matmul(near, jnp.concatenate([c01, c01], axis=0)) + matmul(
            far, jnp.concatenate([c23, c23], axis=0)
        )
        product = (product[:, :64] + product[:, 64:]).reshape(8, 2, 8, 64)
        for odd in range(2):
            stage[:, 64 * odd + 8 * part : 64 * odd + 8 * part + 8, :] = product[:, odd]

    def half_step(step, carry):
        half = 1 - step
        solve(half)

        @pl.when(step == 0)
        def _():
            weights[32] = weights[31]
            weights[33] = jnp.zeros((64, 128), BF16)

        for fh in range(2):
            turn(half, fh)
        for part in range(8):
            blend(half, part)
        for pair in range(8):
            rows = stage[pair].T
            for odd in range(2):
                back[half, pl.ds(pair + 8 * odd, 32, stride=16), :] = rows[
                    32 * odd : 32 * odd + 32
                ]
        over_peers(lambda peer: send_back(half, peer).start())
        keep(half).start()
        return carry

    lax.fori_loop(0, 2, half_step, 0)

    for part in range(2):
        for direction in range(2):
            halo(direction, part).wait_send()
    for direction in range(2):
        to_side(direction).wait_send()
    for rel in range(3):
        arrived(picked_in.at[rel], 15 if rel == 1 else 16, pick_send.at[rel])

    @pl.when(jnp.logical_not(later))
    def _():
        arrived(beyond_in, 15, beyond_send)

    for fh in range(4):
        all_bytes(gathered.at[fh], fore_send.at[fh]).wait()
    for half in range(2):
        all_bytes(back.at[half], back_send.at[half]).wait()
        keep(half).wait()
    for half in range(2):
        all_bytes(back.at[half], back_recv.at[half]).wait()


def place(back_in, out, landed, placed, load_sem, leave_sem):
    lane = lax.broadcasted_iota(jnp.int32, (16, 128), 1)
    flat = landed.reshape(4, 2, 128, 128)

    def load(k):
        return pltpu.make_async_copy(back_in.at[:, :, k], landed.at[k], load_sem.at[k])

    def leave(k):
        return pltpu.make_async_copy(placed.at[k], out.at[k], leave_sem.at[k])

    for k in range(4):
        load(k).start()
    for k in range(4):
        load(k).wait()
        for pair in range(8):
            low, high = [flat[k, half, pl.ds(pair, 16, stride=8), :] for half in range(2)]
            placed[k, 2 * pair] = jnp.where(lane < 64, low, pltpu.roll(high, 64, 1))
            placed[k, 2 * pair + 1] = jnp.where(lane < 64, pltpu.roll(low, 64, 1), high)
        leave(k).start()
    for k in range(4):
        leave(k).wait()


def per_device(background_fields, obs_col, measured_height, obs_radius, obs_value, obs_var):
    dma = pltpu.SemaphoreType.DMA
    result = pl.pallas_call(
        kernel,
        out_shape=jax.ShapeDtypeStruct((2, 512, 128), F32),
        in_specs=[pl.BlockSpec(memory_space=pltpu.HBM)] * 6,
        out_specs=pl.BlockSpec(memory_space=pltpu.HBM),
        scratch_shapes=[
            pltpu.VMEM((1024, 128), F32),
            pltpu.VMEM((16, 128), jnp.int32),
            pltpu.VMEM((16, 128), jnp.int32),
            pltpu.VMEM((1, 64), jnp.int32),
            pltpu.VMEM((1, 64), F32),
            pltpu.VMEM((1, 64), F32),
            pltpu.VMEM((20, 4, 16, 128), F32),
            pltpu.VMEM((18, 4, 16, 128), F32),
            pltpu.VMEM((16, 16, 128), F32),
            pltpu.VMEM((16, 4, 16, 128), F32),
            pltpu.VMEM((4, 256, 128), F32),
            pltpu.VMEM((16, 64, 128), F32),
            pltpu.VMEM((34, 64, 128), BF16),
            pltpu.VMEM((32, 256), F32),
            pltpu.VMEM((64, 256), F32),
            pltpu.VMEM((8, 128), F32),
            pltpu.VMEM((2, 8, 128), F32),
            pltpu.VMEM((2, 128), F32),
            pltpu.VMEM((2, 128), F32),
            pltpu.VMEM((2, 128), F32),
            pltpu.VMEM((2, 16, 128), F32),
            pltpu.VMEM((3, 16, 2, 128), F32),
            pltpu.VMEM((16, 2, 128), F32),
            pltpu.VMEM((8, 128, 64), F32),
            pltpu.VMEM((2, 512, 128), F32),
            dma((6,)),
            dma((4,)),
            dma((4,)),
            dma((2,)),
            dma((2,)),
            dma((3,)),
            dma((3,)),
            dma,
            dma,
            pltpu.SemaphoreType.REGULAR,
            pltpu.SemaphoreType.REGULAR,
            pltpu.SemaphoreType.REGULAR,
            pltpu.SemaphoreType.REGULAR,
            dma((4,)),
            dma((4,)),
            dma((2,)),
            dma((2,)),
            dma((2,)),
        ],
        compiler_params=pltpu.CompilerParams(
            collective_id=0, has_side_effects=True, vmem_limit_bytes=64 * 1024 * 1024
        ),
    )(
        *(
            pltpu.with_memory_space_constraint(x, pltpu.HBM)
            for x in (
                background_fields.reshape(1024, 128),
                obs_col.reshape(16, 128),
                obs_radius.reshape(16, 128),
                measured_height.reshape(1, 64),
                obs_value.reshape(1, 64),
                obs_var.reshape(1, 64),
            )
        )
    )
    return pl.pallas_call(
        place,
        out_shape=jax.ShapeDtypeStruct((4, 16, 16, 128), F32),
        in_specs=[pl.BlockSpec(memory_space=pltpu.HBM)],
        out_specs=pl.BlockSpec(memory_space=pltpu.HBM),
        scratch_shapes=[
            pltpu.VMEM((4, 2, 16, 8, 128), F32),
            pltpu.VMEM((4, 16, 16, 128), F32),
            dma((4,)),
            dma((4,)),
        ],
        compiler_params=pltpu.CompilerParams(vmem_limit_bytes=60 * 1024 * 1024),
    )(result.reshape(2, 16, 4, 8, 128))


def solution(mesh):
    return jax.shard_map(
        per_device,
        mesh=mesh,
        in_specs=(P("member", None, "gx", None), P(), P("gx"), P(), P("gx"), P("gx")),
        out_specs=P("member", None, "gx", None),
        check_vma=False,
    )
```

```python
import jax
import jax.numpy as jnp
from jax import lax
from jax.experimental import pallas as pl
from jax.experimental.pallas import tpu as pltpu
from jax.sharding import PartitionSpec as P

NS_ITERS = 6
COURANT = 0.6
DIFFUSE = 0.1
NS_PAIRS = 8
EARLY = 2
LATER_EARLY = 1
F32 = jnp.float32
BF16 = jnp.bfloat16
MESH = pl.DeviceIdType.MESH


def split2(x):
    hi = x.astype(BF16)
    lo = (x - hi.astype(F32)).astype(BF16)
    return hi, lo


def matmul(a, b):
    return lax.dot_general(a, b, (((1,), (0,)), ((), ())), preferred_element_type=F32)


def matmul_t(a, b):
    return lax.dot_general(a, b, (((1,), (1,)), ((), ())), preferred_element_type=F32)


def advance(west, center, east):
    shape = center.shape
    rows = center.reshape(-1, shape[-1])
    lane = lax.broadcasted_iota(jnp.int32, rows.shape, 1)
    south = jnp.where(lane == 0, 0.0, pltpu.roll(rows, 1, 1)).reshape(shape)
    north = jnp.where(lane == 127, 0.0, pltpu.roll(rows, 127, 1)).reshape(shape)
    return (
        center
        + COURANT * (west - center)
        + DIFFUSE * (west + east + south + north - 4.0 * center)
    )


def kernel(
    bg_hbm,
    col_hbm,
    radius_hbm,
    height_hbm,
    value_hbm,
    var_hbm,
    back_in,
    bg,
    col,
    radius,
    height,
    value,
    var,
    state,
    mid,
    low_fields,
    fore,
    gathered,
    turned,
    weights,
    wgt,
    spread_ref,
    side,
    side_in,
    picked,
    partial,
    beyond,
    edge,
    picked_in,
    beyond_in,
    stage,
    back,
    load_sem,
    halo_send,
    halo_recv,
    side_send,
    side_recv,
    pick_send,
    pick_recv,
    beyond_send,
    beyond_recv,
    ready,
    partner_ready,
    group_in,
    mate_in,
    fore_send,
    fore_recv,
    back_send,
    back_recv,
    keep_sem,
):
    me = lax.axis_index("member")
    tile = lax.axis_index("gx")
    group = 16
    tiles = lax.axis_size("gx")
    right = lax.rem(tile + 1, tiles)
    left = lax.rem(tile + tiles - 1, tiles)

    def load(i):
        pairs = (
            (bg_hbm, bg),
            (value_hbm, value),
            (var_hbm, var),
            (col_hbm, col),
            (height_hbm, height),
            (radius_hbm, radius),
        )
        return pltpu.make_async_copy(*pairs[i], load_sem.at[i])

    for i in range(6):
        load(i).start()

    core = lax.rem(tile, 2)
    later = lax.rem(tile // 2, 2) == 1
    mate = jnp.where(core == 0, right, left)
    across = jnp.where(core == 0, left, right)

    def signal(sem, device):
        pl.semaphore_signal(sem, inc=1, device_id=device, device_id_type=MESH)

    def over_group(action, start=0):
        def body(d, carry):
            action(lax.rem(me + d, group))
            return carry

        lax.fori_loop(start, group, body, 0)

    barrier = pltpu.get_barrier_semaphore()

    @pl.when(later)
    def _():
        signal(barrier, {"gx": mate})

    @pl.when(jnp.logical_not(later))
    def _():
        over_group(lambda peer: signal(barrier, {"member": peer, "gx": across}))
        over_group(lambda peer: signal(barrier, {"member": peer}), 1)
        over_group(lambda peer: signal(barrier, {"member": peer, "gx": mate}))

    for i in range(6):
        load(i).wait()

    def rearrange(x, carry):
        for k in range(4):
            rows = bg[pl.ds(k * 256 + x, 16, stride=16), :]
            for fh in range(4):
                state[x + 2, fh, 4 * k : 4 * k + 4, :] = rows[4 * fh : 4 * fh + 4]
        return carry

    lax.fori_loop(0, 16, rearrange, 0)
    side[...] = jnp.concatenate(
        [
            jnp.concatenate([value[...], var[...]], axis=1),
            jnp.concatenate([height[...].astype(F32), jnp.zeros((1, 64), F32)], axis=1),
            jnp.zeros((6, 128), F32),
        ],
        axis=0,
    )

    @pl.when(jnp.logical_not(later))
    def _():
        pl.semaphore_wait(barrier, 2 * group - 1)

    @pl.when(later)
    def _():
        pl.semaphore_wait(barrier, group + 1)
        signal(partner_ready, {"gx": across})

    def halo(direction, part):
        which = pl.ds(0, 1) if part == 0 else pl.ds(1, 3)
        src, dst, peer = ((16, 0, right), (2, 18, left))[direction]
        slot = direction * 2 + part
        return pltpu.make_async_remote_copy(
            src_ref=state.at[pl.ds(src, 2), which],
            dst_ref=state.at[pl.ds(dst, 2), which],
            send_sem=halo_send.at[slot],
            recv_sem=halo_recv.at[slot],
            device_id={"gx": peer},
            device_id_type=MESH,
        )

    def to_side(direction):
        return pltpu.make_async_remote_copy(
            src_ref=side,
            dst_ref=side_in.at[direction],
            send_sem=side_send.at[direction],
            recv_sem=side_recv.at[direction],
            device_id={"gx": (right, left)[direction]},
            device_id_type=MESH,
        )

    def to_mate():
        for direction in range(2):

            @pl.when(core == direction)
            def _():
                halo(direction, 0).start()
                to_side(direction).start()
                halo(direction, 1).start()

    def to_across():
        for direction in range(2):

            @pl.when(core != direction)
            def _():
                halo(direction, 0).start()
                to_side(direction).start()
                halo(direction, 1).start()

    @pl.when(later)
    def _():
        to_across()
        over_group(lambda peer: signal(ready, {"member": peer, "gx": across}), 1)

    to_mate()

    def first_step(index, which):
        mid[index, which] = advance(
            state[index, which], state[index + 1, which], state[index + 2, which]
        )

    def second_step(x, which):
        return advance(mid[x, which], mid[x + 1, which], mid[x + 2, which])

    def pack(x, fields):
        is_left = lax.broadcasted_iota(jnp.int32, (16, 128), 1) < 64
        for fh in range(2):
            a, b = fields[fh], fields[fh + 2]
            fore[x, fh] = jnp.where(is_left, pltpu.roll(a, 64, 1), b)
            fore[x, 2 + fh] = jnp.where(is_left, a, pltpu.roll(b, 64, 1))


    def inner_rows(part):
        which = pl.ds(0, 1) if part == 0 else pl.ds(1, 3)

        def inner_first(i, carry):
            for j in range(7):
                first_step(2 + 7 * i + j, which)
            return carry

        def inner_second(i, carry):
            for j in range(6):
                x = 2 + 6 * i + j
                fields = second_step(x, which)
                if part == 0:
                    low_fields[x] = fields[0]
                else:
                    pack(x, [low_fields[x], fields[0], fields[1], fields[2]])
            return carry

        lax.fori_loop(0, 2, inner_first, 0)
        lax.fori_loop(0, 2, inner_second, 0)

    def send_fore(piece, peer):
        return pltpu.make_async_remote_copy(
            src_ref=fore.at[peer, piece],
            dst_ref=gathered.at[piece, pl.ds(pl.multiple_of(me * 16, 16), 16), :],
            send_sem=fore_send.at[piece],
            recv_sem=fore_recv.at[piece],
            device_id={"member": peer},
            device_id_type=MESH,
        )

    def over_peers(action):
        over_group(action, 1)

    def start_fore(inner_pieces, outer_pieces):
        def body(peer):
            is_inner = (peer >= 2) & (peer < 14)

            @pl.when(is_inner)
            def _():
                for piece in inner_pieces:
                    send_fore(piece, peer).start()

            @pl.when(jnp.logical_not(is_inner))
            def _():
                for piece in outer_pieces:
                    send_fore(piece, peer).start()

        over_peers(body)

    def edge_rows(part, direction):
        which = pl.ds(0, 1) if part == 0 else pl.ds(1, 3)
        count = 1 if part == 0 else 3
        halo(direction, part).wait_recv()
        nothing = jnp.zeros((count, 16, 128), F32)
        outside = tile == (0, tiles - 1)[direction]
        slots, firsts, seconds, beyond = (
            ((0, 1), (0, 1), (0, 1), 0),
            ((18, 19), (16, 17), (14, 15), 17),
        )[direction]

        @pl.when(outside)
        def _():
            for slot in slots:
                state[slot, which] = nothing

        for index in firsts:
            first_step(index, which)

        @pl.when(outside)
        def _():
            mid[beyond, which] = nothing

        for x in seconds:
            fields = second_step(x, which)
            if part == 0:
                low_fields[x] = fields[0]
            else:
                pack(x, [low_fields[x], fields[0], fields[1], fields[2]])

    def tile_row(ref, t):
        row = ref[pl.ds(t // 2, 1), :]
        return jnp.where(lax.rem(t, 2) == 0, row[:, :64], row[:, 64:])

    def hot(column):
        rows = lax.broadcasted_iota(jnp.int32, (128, 64), 0)
        return (rows == lax.rem(column, 128)).astype(F32).astype(BF16)

    def sample(rows, hot_y, along, levels):
        observed = jnp.concatenate(rows, axis=0)
        hi, lo = split2(observed)
        low = (observed - hi.astype(F32) - lo.astype(F32)).astype(BF16)
        along_y = (matmul(hi, hot_y) + matmul(lo, hot_y)) + matmul(low, hot_y)
        total = jnp.zeros((16, 64), F32)
        for i, x in enumerate(along[1]):
            total = total + jnp.where(along[0] == x, along_y[16 * i : 16 * i + 16], 0.0)
        level = lax.rem(lax.broadcasted_iota(jnp.int32, (16, 64), 0), 4)
        total = jnp.where(level == levels, total, 0.0)
        sums = [jnp.sum(total[4 * k : 4 * k + 4], axis=0, keepdims=True) for k in range(4)]
        return jnp.concatenate(
            [
                jnp.concatenate([sums[0], sums[1]], axis=1),
                jnp.concatenate([sums[2], sums[3]], axis=1),
            ],
            axis=0,
        )

    own_col = tile_row(col, tile)
    own_x = own_col // 128 - tile * 16
    hot_own = hot(own_col)

    def own_samples():
        rows = [low_fields[x] for x in range(16)]
        return sample(rows, hot_own, (own_x, range(16)), height[...])

    def send_picked(buffer, rel, device):
        return pltpu.make_async_remote_copy(
            src_ref=buffer,
            dst_ref=picked_in.at[rel, me],
            send_sem=pick_send.at[rel],
            recv_sem=pick_recv.at[rel],
            device_id=device,
            device_id_type=MESH,
        )

    def send_beyond(device):
        return pltpu.make_async_remote_copy(
            src_ref=beyond,
            dst_ref=beyond_in.at[me],
            send_sem=beyond_send,
            recv_sem=beyond_recv,
            device_id=device,
            device_id_type=MESH,
        )

    def over_tile(rel, action):
        def body(d, carry):
            peer = lax.rem(me + d, group)
            action({"member": peer} if rel == 1 else {"member": peer, "gx": (right, 0, left)[rel]})
            return carry

        lax.fori_loop(1 if rel == 1 else 0, group, body, 0)

    inner_rows(0)

    @pl.when(jnp.logical_not(later))
    def _():
        inner_rows(1)
        start_fore(range(EARLY), ())
        pl.semaphore_wait(partner_ready, 1)
        to_across()

    none = jnp.zeros((16, 128), F32)

    @pl.when(core == 0)
    def _():
        edge_rows(0, 1)
        first, second = state[2, 0], state[3, 0]
        outer, inner = advance(none, none, first), advance(none, first, second)
        low_fields[0] = advance(outer, inner, mid[2, 0])
        low_fields[1] = advance(inner, mid[2, 0], mid[3, 0])
        edge[0] = advance(none, none, outer)
        edge[1] = advance(none, outer, inner)

    @pl.when(core == 1)
    def _():
        edge_rows(0, 0)
        first, second = state[17, 0], state[16, 0]
        outer, inner = advance(first, none, none), advance(second, first, none)
        low_fields[15] = advance(mid[15, 0], inner, outer)
        low_fields[14] = advance(mid[14, 0], mid[15, 0], inner)
        edge[0] = advance(inner, outer, none)
        edge[1] = advance(outer, none, none)

    @pl.when(later)
    def _():
        partial[...] = own_samples()

        @pl.when(core == 0)
        def _():
            over_tile(2, lambda device: send_picked(partial, 2, device).start())

        @pl.when(core == 1)
        def _():
            over_tile(0, lambda device: send_picked(partial, 0, device).start())

    @pl.when(later)
    def _():
        inner_rows(1)
        pl.semaphore_wait(group_in, 1)
        signal(mate_in, {"gx": mate})
        start_fore(range(LATER_EARLY), ())
        pl.semaphore_wait(mate_in, 1)

    @pl.when(jnp.logical_not(later))
    def _():
        pl.semaphore_wait(ready, group - 1)
        signal(group_in, {"gx": across})

    @pl.when(core == 0)
    def _():
        edge_rows(0, 0)

    @pl.when(core == 1)
    def _():
        edge_rows(0, 1)

    for direction in range(2):
        to_side(direction).wait_recv()
    picked[...] = own_samples()
    over_tile(1, lambda device: send_picked(picked, 1, device).start())

    @pl.when(core == 0)
    def _():
        over_tile(0, lambda device: send_picked(picked, 0, device).start())

    @pl.when(core == 1)
    def _():
        over_tile(2, lambda device: send_picked(picked, 2, device).start())

    @pl.when(jnp.logical_not(later))
    def _():
        across_col = tile_row(col, across)
        across_x = across_col // 128 - across * 16 - jnp.where(core == 0, 14, 0)
        levels = jnp.where(core == 0, side_in[0, 1:2, :64], side_in[1, 1:2, :64])
        beyond[...] = sample(
            [edge[0], edge[1]],
            hot(across_col),
            (across_x, range(2)),
            levels.astype(jnp.int32),
        )
        beyond_in[me] = beyond[...]
        over_tile(1, lambda device: send_beyond(device).start())

        @pl.when(core == 0)
        def _():
            over_tile(2, lambda device: send_picked(picked, 2, device).start())

        @pl.when(core == 1)
        def _():
            over_tile(0, lambda device: send_picked(picked, 0, device).start())

    @pl.when(later)
    def _():
        beyond_in[...] = jnp.zeros((16, 2, 128), F32)

    picked_in[1, me] = picked[...]

    @pl.when(later)
    def _():
        start_fore(range(LATER_EARLY, 2), ())

    if EARLY < 2:

        @pl.when(jnp.logical_not(later))
        def _():
            start_fore(range(EARLY, 2), ())

    for direction in range(2):
        edge_rows(1, direction)
    start_fore((), range(2))

    @pl.when(later)
    def _():
        start_fore(range(2, 4), range(2, 4))

    @pl.when(jnp.logical_not(later))
    def _():
        start_fore(range(max(EARLY, 2), 4), range(2, 4))

    gathered[:, pl.ds(pl.multiple_of(me * 16, 16), 16), :] = fore[me]

    def three(a, b, c, fill):
        return jnp.concatenate([a, b, c, jnp.full((1, 64), fill, a.dtype)], axis=1)

    before = jnp.maximum(tile - 1, 0)
    after = jnp.minimum(tile + 1, tiles - 1)
    near_col = three(tile_row(col, before), own_col, tile_row(col, after), 0)
    near_radius = three(
        tile_row(radius, before), tile_row(radius, tile), tile_row(radius, after), 1
    ).astype(F32)
    from_left, own, from_right = side_in[0, 0:1, :], side[0:1, :], side_in[1, 0:1, :]
    near_value = three(from_left[:, :64], own[:, :64], from_right[:, :64], 0.0)
    near_var = three(from_left[:, 64:], own[:, 64:], from_right[:, 64:], 1.0)
    lane = lax.broadcasted_iota(jnp.int32, (1, 256), 1)
    first = jnp.where(tile == 0, 64, 0)
    last = jnp.where(tile == tiles - 1, 128, 192)
    valid = (lane >= first) & (lane < last)
    inverse = jnp.where(valid, 1.0 / near_var, 0.0)
    gap_along = (tile * 16 + me - near_col // 128).astype(F32)
    site = 4 * lax.broadcasted_iota(jnp.int32, (32, 256), 0)
    gap_across = (site - lax.rem(near_col, 128)).astype(F32)
    taper = jnp.maximum(
        0.0,
        1.0 - (gap_along * gap_along + gap_across * gap_across) / (near_radius * near_radius),
    )
    wgt[...] = taper * inverse

    def arrived(buffer, count, sem):
        rows = buffer.at[pl.ds(0, count)]
        pltpu.make_async_copy(rows, rows, sem).wait()

    def by_member(buffer):
        rows = jnp.concatenate([buffer[m] for m in range(16)], axis=0)
        return jnp.concatenate([rows[:, :64], rows[:, 64:]], axis=0)

    for rel in range(3):
        arrived(picked_in.at[rel], 15 if rel == 1 else 16, pick_recv.at[rel])

    @pl.when(jnp.logical_not(later))
    def _():
        arrived(beyond_in, 15, beyond_recv)

    added = by_member(beyond_in)
    ensemble = jnp.concatenate(
        [
            by_member(picked_in.at[0]) + jnp.where(core == 0, added, 0.0),
            by_member(picked_in.at[1]),
            by_member(picked_in.at[2]) + jnp.where(core == 1, added, 0.0),
            jnp.zeros((64, 64), F32),
        ],
        axis=1,
    )
    mean = jnp.sum(ensemble, axis=0, keepdims=True) / 64.0
    spread = ensemble - mean
    innovation = near_value - mean
    spread_ref[...] = spread
    spread_hi, spread_lo = split2(spread)
    across_obs = jnp.concatenate([spread_hi, spread_hi, spread_lo, spread_lo], axis=0)

    lane2 = lax.broadcasted_iota(jnp.int32, (64, 128), 1)
    row2 = lax.broadcasted_iota(jnp.int32, (64, 128), 0)
    is_first = lane2 < 64
    eye = (lax.rem(lane2, 64) == row2).astype(F32)
    is_first_row = lax.broadcasted_iota(jnp.int32, (1, 128), 1) < 64

    def operand(x):
        hi, lo = split2(x)
        return jnp.concatenate([hi, lo], axis=1)

    def stationary(x):
        hi = x.astype(BF16).astype(F32)
        lo = x - hi
        zero = jnp.zeros_like(x)
        top = jnp.concatenate(
            [jnp.where(is_first, hi, zero), jnp.where(is_first, lo, zero)], axis=1
        ).astype(BF16)
        bottom = jnp.concatenate(
            [jnp.where(is_first, zero, hi), jnp.where(is_first, zero, lo)], axis=1
        ).astype(BF16)
        return jnp.concatenate([top, bottom, top, bottom], axis=0)

    def fold(x):
        return x[:, :128] + x[:, 128:]

    def solve(batch):
        pairs = [batch * NS_PAIRS + i for i in range(NS_PAIRS)]
        system, drive = [], []
        for p in pairs:
            scaled = [spread_ref[...] * wgt[pl.ds(2 * p + h, 1), :] for h in range(2)]
            both = jnp.concatenate(scaled, axis=0)
            hi, lo = split2(both)
            product = fold(matmul_t(hi, across_obs)) + matmul_t(lo, across_obs[:128])
            system.append(jnp.where(is_first, product[:64], product[64:]) + 63.0 * eye)
            sums = [jnp.sum(s * innovation, axis=1, keepdims=True) for s in scaled]
            drive.append(jnp.where(is_first, sums[0], sums[1]))
        inv_norm, power, root = [], [], []
        for s in system:
            squares = jnp.sum(s * s, axis=0, keepdims=True)
            one = jnp.sum(jnp.where(is_first_row, squares, 0.0), axis=1, keepdims=True)
            two = jnp.sum(jnp.where(is_first_row, 0.0, squares), axis=1, keepdims=True)
            inv = 1.0 / jnp.sqrt(jnp.where(is_first_row, one, two))
            inv_norm.append(inv)
            power.append(s * inv)
        root = [1.5 * eye - 0.5 * p for p in power]
        for sweep in range(NS_ITERS - 1):
            fixed = [stationary(p) for p in power]
            moving = [operand(p) for p in power]
            if sweep == 0:
                square = [fold(matmul(m, f)) for m, f in zip(moving, fixed)]
            else:
                stacked = [
                    fold(matmul(jnp.concatenate([m, operand(z)], axis=0), f))
                    for m, z, f in zip(moving, root, fixed)
                ]
                square = [s[:64] for s in stacked]
                root = [1.5 * z - 0.5 * s[64:] for z, s in zip(root, stacked)]
            cube = [fold(matmul(operand(s), f)) for s, f in zip(square, fixed)]
            power = [2.25 * p - 1.5 * s + 0.25 * c for p, s, c in zip(power, square, cube)]
        root = [
            1.5 * z - 0.5 * fold(matmul(operand(z), stationary(p))) for z, p in zip(root, power)
        ]
        for p, z, inv, d in zip(pairs, root, inv_norm, drive):
            through = jnp.sum(z * d, axis=0, keepdims=True)
            again = z * through
            one = jnp.sum(jnp.where(is_first, again, 0.0), axis=1, keepdims=True)
            two = jnp.sum(jnp.where(is_first, 0.0, again), axis=1, keepdims=True)
            w = jnp.sqrt(63.0 * inv) * z + jnp.where(is_first, one, two) * inv
            w = w + (1.0 - jnp.sum(w, axis=0, keepdims=True)) * (1.0 / 64.0)
            hi = w.astype(BF16).astype(F32)
            lo = w - hi
            weights[2 * p] = jnp.where(is_first, hi, pltpu.roll(lo, 64, 1)).astype(BF16)
            weights[2 * p + 1] = jnp.where(is_first, pltpu.roll(hi, 64, 1), lo).astype(BF16)

    y8 = lax.broadcasted_iota(jnp.int32, (1, 8, 128), 1).astype(F32) * 0.25
    half = lax.broadcasted_iota(jnp.int32, (1, 8, 128), 2) < 64
    tent = [jnp.maximum(0.0, 1.0 - jnp.abs(y8 - c)) for c in range(3)]
    coef_a = jnp.where(half, tent[0], tent[1])
    coef_b = jnp.where(half, tent[2], 0.0)

    def all_bytes(buffer, sem):
        rows = buffer.at[pl.ds(0, buffer.shape[0] // group * (group - 1))]
        return pltpu.make_async_copy(rows, rows, sem)

    def send_back(half, peer):
        return pltpu.make_async_remote_copy(
            src_ref=back.at[half, pl.ds(pl.multiple_of(peer * 32, 32), 32), :],
            dst_ref=back_in.at[half, pl.ds(pl.multiple_of(me * 32, 32), 32), :],
            send_sem=back_send.at[half],
            recv_sem=back_recv.at[half],
            device_id={"member": peer},
            device_id_type=MESH,
        )

    def keep(half):
        rows = pl.ds(pl.multiple_of(me * 32, 32), 32)
        return pltpu.make_async_copy(
            back.at[half, rows], back_in.at[half, rows], keep_sem.at[half]
        )

    def turn(half, fh):
        piece = 2 * (1 - half) + fh
        all_bytes(gathered.at[piece], fore_recv.at[piece]).wait()
        for fl in range(4):
            rows = jnp.concatenate(
                [gathered[piece, pl.ds(fl + 4 * odd, 32, stride=8), :] for odd in range(2)], axis=0
            )
            columns = jnp.concatenate([rows, rows], axis=0).T
            turned[4 * fh + fl] = columns[:64]
            turned[8 + 4 * fh + fl] = columns[64:]

    def blend(half, part):
        block = half * 8 + part
        rows = turned[:, 8 * part : 8 * part + 8, :]
        near = operand((rows * coef_a).reshape(128, 128))
        far = operand((rows * coef_b).reshape(128, 128))
        c01 = weights[pl.ds(2 * block, 2)].reshape(128, 128)
        c23 = weights[pl.ds(2 * block + 2, 2)].reshape(128, 128)
        product = matmul(near, jnp.concatenate([c01, c01], axis=0)) + matmul(
            far, jnp.concatenate([c23, c23], axis=0)
        )
        product = (product[:, :64] + product[:, 64:]).reshape(8, 2, 8, 64)
        for odd in range(2):
            stage[:, 64 * odd + 8 * part : 64 * odd + 8 * part + 8, :] = product[:, odd]

    def half_step(step, carry):
        half = 1 - step
        solve(half)

        @pl.when(step == 0)
        def _():
            weights[32] = weights[31]
            weights[33] = jnp.zeros((64, 128), BF16)

        for fh in range(2):
            turn(half, fh)
        for part in range(8):
            blend(half, part)
        for pair in range(8):
            rows = stage[pair].T
            for odd in range(2):
                back[half, pl.ds(pair + 8 * odd, 32, stride=16), :] = rows[
                    32 * odd : 32 * odd + 32
                ]
        over_peers(lambda peer: send_back(half, peer).start())
        keep(half).start()
        return carry

    lax.fori_loop(0, 2, half_step, 0)

    for part in range(2):
        for direction in range(2):
            halo(direction, part).wait_send()
    for direction in range(2):
        to_side(direction).wait_send()
    for rel in range(3):
        arrived(picked_in.at[rel], 15 if rel == 1 else 16, pick_send.at[rel])

    @pl.when(jnp.logical_not(later))
    def _():
        arrived(beyond_in, 15, beyond_send)

    for fh in range(4):
        all_bytes(gathered.at[fh], fore_send.at[fh]).wait()
    for half in range(2):
        all_bytes(back.at[half], back_send.at[half]).wait()
        keep(half).wait()
    for half in range(2):
        all_bytes(back.at[half], back_recv.at[half]).wait()


def place(back_in, out, landed, placed, load_sem, leave_sem):
    lane = lax.broadcasted_iota(jnp.int32, (16, 128), 1)
    flat = landed.reshape(4, 2, 128, 128)

    def load(k):
        return pltpu.make_async_copy(back_in.at[:, :, k], landed.at[k], load_sem.at[k])

    def leave(k):
        return pltpu.make_async_copy(placed.at[k], out.at[k], leave_sem.at[k])

    for k in range(4):
        load(k).start()
    for k in range(4):
        load(k).wait()
        for pair in range(8):
            low, high = [flat[k, half, pl.ds(pair, 16, stride=8), :] for half in range(2)]
            placed[k, 2 * pair] = jnp.where(lane < 64, low, pltpu.roll(high, 64, 1))
            placed[k, 2 * pair + 1] = jnp.where(lane < 64, pltpu.roll(low, 64, 1), high)
        leave(k).start()
    for k in range(4):
        leave(k).wait()


def per_device(background_fields, obs_col, measured_height, obs_radius, obs_value, obs_var):
    dma = pltpu.SemaphoreType.DMA
    result = pl.pallas_call(
        kernel,
        out_shape=jax.ShapeDtypeStruct((2, 512, 128), F32),
        in_specs=[pl.BlockSpec(memory_space=pltpu.HBM)] * 6,
        out_specs=pl.BlockSpec(memory_space=pltpu.HBM),
        scratch_shapes=[
            pltpu.VMEM((1024, 128), F32),
            pltpu.VMEM((16, 128), jnp.int32),
            pltpu.VMEM((16, 128), jnp.int32),
            pltpu.VMEM((1, 64), jnp.int32),
            pltpu.VMEM((1, 64), F32),
            pltpu.VMEM((1, 64), F32),
            pltpu.VMEM((20, 4, 16, 128), F32),
            pltpu.VMEM((18, 4, 16, 128), F32),
            pltpu.VMEM((16, 16, 128), F32),
            pltpu.VMEM((16, 4, 16, 128), F32),
            pltpu.VMEM((4, 256, 128), F32),
            pltpu.VMEM((16, 64, 128), F32),
            pltpu.VMEM((34, 64, 128), BF16),
            pltpu.VMEM((32, 256), F32),
            pltpu.VMEM((64, 256), F32),
            pltpu.VMEM((8, 128), F32),
            pltpu.VMEM((2, 8, 128), F32),
            pltpu.VMEM((2, 128), F32),
            pltpu.VMEM((2, 128), F32),
            pltpu.VMEM((2, 128), F32),
            pltpu.VMEM((2, 16, 128), F32),
            pltpu.VMEM((3, 16, 2, 128), F32),
            pltpu.VMEM((16, 2, 128), F32),
            pltpu.VMEM((8, 128, 64), F32),
            pltpu.VMEM((2, 512, 128), F32),
            dma((6,)),
            dma((4,)),
            dma((4,)),
            dma((2,)),
            dma((2,)),
            dma((3,)),
            dma((3,)),
            dma,
            dma,
            pltpu.SemaphoreType.REGULAR,
            pltpu.SemaphoreType.REGULAR,
            pltpu.SemaphoreType.REGULAR,
            pltpu.SemaphoreType.REGULAR,
            dma((4,)),
            dma((4,)),
            dma((2,)),
            dma((2,)),
            dma((2,)),
        ],
        compiler_params=pltpu.CompilerParams(
            collective_id=0, has_side_effects=True, vmem_limit_bytes=64 * 1024 * 1024
        ),
    )(
        *(
            pltpu.with_memory_space_constraint(x, pltpu.HBM)
            for x in (
                background_fields.reshape(1024, 128),
                obs_col.reshape(16, 128),
                obs_radius.reshape(16, 128),
                measured_height.reshape(1, 64),
                obs_value.reshape(1, 64),
                obs_var.reshape(1, 64),
            )
        )
    )
    return pl.pallas_call(
        place,
        out_shape=jax.ShapeDtypeStruct((4, 16, 16, 128), F32),
        in_specs=[pl.BlockSpec(memory_space=pltpu.HBM)],
        out_specs=pl.BlockSpec(memory_space=pltpu.HBM),
        scratch_shapes=[
            pltpu.VMEM((4, 2, 16, 8, 128), F32),
            pltpu.VMEM((4, 16, 16, 128), F32),
            dma((4,)),
            dma((4,)),
        ],
        compiler_params=pltpu.CompilerParams(vmem_limit_bytes=60 * 1024 * 1024),
    )(result.reshape(2, 16, 4, 8, 128))


def solution(mesh):
    return jax.shard_map(
        per_device,
        mesh=mesh,
        in_specs=(P("member", None, "gx", None), P(), P("gx"), P(), P("gx"), P("gx")),
        out_specs=P("member", None, "gx", None),
        check_vma=False,
    )
```

```python
import jax
import jax.numpy as jnp
from jax import lax
from jax.experimental import pallas as pl
from jax.experimental.pallas import tpu as pltpu
from jax.sharding import PartitionSpec as P

NS_ITERS = 6
COURANT = 0.6
DIFFUSE = 0.1
NS_PAIRS = 8
EARLY = 2
LATER_EARLY = 1
F32 = jnp.float32
BF16 = jnp.bfloat16
MESH = pl.DeviceIdType.MESH


def split2(x):
    hi = x.astype(BF16)
    lo = (x - hi.astype(F32)).astype(BF16)
    return hi, lo


def matmul(a, b):
    return lax.dot_general(a, b, (((1,), (0,)), ((), ())), preferred_element_type=F32)


def matmul_t(a, b):
    return lax.dot_general(a, b, (((1,), (1,)), ((), ())), preferred_element_type=F32)


def advance(west, center, east):
    shape = center.shape
    rows = center.reshape(-1, shape[-1])
    lane = lax.broadcasted_iota(jnp.int32, rows.shape, 1)
    south = jnp.where(lane == 0, 0.0, pltpu.roll(rows, 1, 1)).reshape(shape)
    north = jnp.where(lane == 127, 0.0, pltpu.roll(rows, 127, 1)).reshape(shape)
    return (
        center
        + COURANT * (west - center)
        + DIFFUSE * (west + east + south + north - 4.0 * center)
    )


def kernel(
    bg_hbm,
    col_hbm,
    radius_hbm,
    height_hbm,
    value_hbm,
    var_hbm,
    back_in,
    bg,
    col,
    radius,
    height,
    value,
    var,
    state,
    mid,
    low_fields,
    fore,
    gathered,
    turned,
    weights,
    wgt,
    spread_ref,
    side,
    side_in,
    picked,
    partial,
    beyond,
    edge,
    picked_in,
    beyond_in,
    stage,
    back,
    load_sem,
    halo_send,
    halo_recv,
    side_send,
    side_recv,
    pick_send,
    pick_recv,
    beyond_send,
    beyond_recv,
    ready,
    partner_ready,
    group_in,
    mate_in,
    fore_send,
    fore_recv,
    back_send,
    back_recv,
    keep_sem,
):
    me = lax.axis_index("member")
    tile = lax.axis_index("gx")
    group = 16
    tiles = lax.axis_size("gx")
    right = lax.rem(tile + 1, tiles)
    left = lax.rem(tile + tiles - 1, tiles)

    def load(i):
        pairs = (
            (bg_hbm, bg),
            (value_hbm, value),
            (var_hbm, var),
            (col_hbm, col),
            (height_hbm, height),
            (radius_hbm, radius),
        )
        return pltpu.make_async_copy(*pairs[i], load_sem.at[i])

    for i in range(6):
        load(i).start()

    core = lax.rem(tile, 2)
    later = lax.rem(tile // 2, 2) == 1
    mate = jnp.where(core == 0, right, left)
    across = jnp.where(core == 0, left, right)

    def signal(sem, device):
        pl.semaphore_signal(sem, inc=1, device_id=device, device_id_type=MESH)

    def over_group(action, start=0):
        def body(d, carry):
            action(lax.rem(me + d, group))
            return carry

        lax.fori_loop(start, group, body, 0)

    barrier = pltpu.get_barrier_semaphore()

    @pl.when(later)
    def _():
        signal(barrier, {"gx": mate})
        pl.semaphore_wait(barrier, group + 1)
        signal(partner_ready, {"gx": across})
        over_group(lambda peer: signal(ready, {"member": peer, "gx": across}), 1)

    @pl.when(jnp.logical_not(later))
    def _():
        over_group(lambda peer: signal(barrier, {"member": peer, "gx": across}))
        over_group(lambda peer: signal(barrier, {"member": peer}), 1)
        over_group(lambda peer: signal(barrier, {"member": peer, "gx": mate}))

    for i in range(6):
        load(i).wait()

    def rearrange(x, carry):
        for k in range(4):
            rows = bg[pl.ds(k * 256 + x, 16, stride=16), :]
            for fh in range(4):
                state[x + 2, fh, 4 * k : 4 * k + 4, :] = rows[4 * fh : 4 * fh + 4]
        return carry

    lax.fori_loop(0, 16, rearrange, 0)
    side[...] = jnp.concatenate(
        [
            jnp.concatenate([value[...], var[...]], axis=1),
            jnp.concatenate([height[...].astype(F32), jnp.zeros((1, 64), F32)], axis=1),
            jnp.zeros((6, 128), F32),
        ],
        axis=0,
    )

    @pl.when(jnp.logical_not(later))
    def _():
        pl.semaphore_wait(barrier, 2 * group - 1)

    def halo(direction, part):
        which = pl.ds(0, 1) if part == 0 else pl.ds(1, 3)
        src, dst, peer = ((16, 0, right), (2, 18, left))[direction]
        slot = direction * 2 + part
        return pltpu.make_async_remote_copy(
            src_ref=state.at[pl.ds(src, 2), which],
            dst_ref=state.at[pl.ds(dst, 2), which],
            send_sem=halo_send.at[slot],
            recv_sem=halo_recv.at[slot],
            device_id={"gx": peer},
            device_id_type=MESH,
        )

    def to_side(direction):
        return pltpu.make_async_remote_copy(
            src_ref=side,
            dst_ref=side_in.at[direction],
            send_sem=side_send.at[direction],
            recv_sem=side_recv.at[direction],
            device_id={"gx": (right, left)[direction]},
            device_id_type=MESH,
        )

    def to_mate():
        for direction in range(2):

            @pl.when(core == direction)
            def _():
                halo(direction, 0).start()
                to_side(direction).start()
                halo(direction, 1).start()

    def to_across():
        for direction in range(2):

            @pl.when(core != direction)
            def _():
                halo(direction, 0).start()
                to_side(direction).start()
                halo(direction, 1).start()

    @pl.when(later)
    def _():
        to_across()

    to_mate()

    def first_step(index, which):
        mid[index, which] = advance(
            state[index, which], state[index + 1, which], state[index + 2, which]
        )

    def second_step(x, which):
        return advance(mid[x, which], mid[x + 1, which], mid[x + 2, which])

    def pack(x, fields):
        is_left = lax.broadcasted_iota(jnp.int32, (16, 128), 1) < 64
        for fh in range(2):
            a, b = fields[fh], fields[fh + 2]
            fore[x, fh] = jnp.where(is_left, pltpu.roll(a, 64, 1), b)
            fore[x, 2 + fh] = jnp.where(is_left, a, pltpu.roll(b, 64, 1))


    def inner_rows(part):
        which = pl.ds(0, 1) if part == 0 else pl.ds(1, 3)

        def inner_first(i, carry):
            for j in range(7):
                first_step(2 + 7 * i + j, which)
            return carry

        def inner_second(i, carry):
            for j in range(6):
                x = 2 + 6 * i + j
                fields = second_step(x, which)
                if part == 0:
                    low_fields[x] = fields[0]
                else:
                    pack(x, [low_fields[x], fields[0], fields[1], fields[2]])
            return carry

        lax.fori_loop(0, 2, inner_first, 0)
        lax.fori_loop(0, 2, inner_second, 0)

    def send_fore(piece, peer):
        return pltpu.make_async_remote_copy(
            src_ref=fore.at[peer, piece],
            dst_ref=gathered.at[piece, pl.ds(pl.multiple_of(me * 16, 16), 16), :],
            send_sem=fore_send.at[piece],
            recv_sem=fore_recv.at[piece],
            device_id={"member": peer},
            device_id_type=MESH,
        )

    def over_peers(action):
        over_group(action, 1)

    def start_fore(inner_pieces, outer_pieces):
        def body(peer):
            is_inner = (peer >= 2) & (peer < 14)

            @pl.when(is_inner)
            def _():
                for piece in inner_pieces:
                    send_fore(piece, peer).start()

            @pl.when(jnp.logical_not(is_inner))
            def _():
                for piece in outer_pieces:
                    send_fore(piece, peer).start()

        over_peers(body)

    def edge_rows(part, direction):
        which = pl.ds(0, 1) if part == 0 else pl.ds(1, 3)
        count = 1 if part == 0 else 3
        halo(direction, part).wait_recv()
        nothing = jnp.zeros((count, 16, 128), F32)
        outside = tile == (0, tiles - 1)[direction]
        slots, firsts, seconds, beyond = (
            ((0, 1), (0, 1), (0, 1), 0),
            ((18, 19), (16, 17), (14, 15), 17),
        )[direction]

        @pl.when(outside)
        def _():
            for slot in slots:
                state[slot, which] = nothing

        for index in firsts:
            first_step(index, which)

        @pl.when(outside)
        def _():
            mid[beyond, which] = nothing

        for x in seconds:
            fields = second_step(x, which)
            if part == 0:
                low_fields[x] = fields[0]
            else:
                pack(x, [low_fields[x], fields[0], fields[1], fields[2]])

    def tile_row(ref, t):
        row = ref[pl.ds(t // 2, 1), :]
        return jnp.where(lax.rem(t, 2) == 0, row[:, :64], row[:, 64:])

    def hot(column):
        rows = lax.broadcasted_iota(jnp.int32, (128, 64), 0)
        return (rows == lax.rem(column, 128)).astype(F32).astype(BF16)

    def sample(rows, hot_y, along, levels):
        observed = jnp.concatenate(rows, axis=0)
        hi, lo = split2(observed)
        low = (observed - hi.astype(F32) - lo.astype(F32)).astype(BF16)
        along_y = (matmul(hi, hot_y) + matmul(lo, hot_y)) + matmul(low, hot_y)
        total = jnp.zeros((16, 64), F32)
        for i, x in enumerate(along[1]):
            total = total + jnp.where(along[0] == x, along_y[16 * i : 16 * i + 16], 0.0)
        level = lax.rem(lax.broadcasted_iota(jnp.int32, (16, 64), 0), 4)
        total = jnp.where(level == levels, total, 0.0)
        sums = [jnp.sum(total[4 * k : 4 * k + 4], axis=0, keepdims=True) for k in range(4)]
        return jnp.concatenate(
            [
                jnp.concatenate([sums[0], sums[1]], axis=1),
                jnp.concatenate([sums[2], sums[3]], axis=1),
            ],
            axis=0,
        )

    own_col = tile_row(col, tile)
    own_x = own_col // 128 - tile * 16
    hot_own = hot(own_col)

    def own_samples():
        rows = [low_fields[x] for x in range(16)]
        return sample(rows, hot_own, (own_x, range(16)), height[...])

    def send_picked(buffer, rel, device):
        return pltpu.make_async_remote_copy(
            src_ref=buffer,
            dst_ref=picked_in.at[rel, me],
            send_sem=pick_send.at[rel],
            recv_sem=pick_recv.at[rel],
            device_id=device,
            device_id_type=MESH,
        )

    def send_beyond(device):
        return pltpu.make_async_remote_copy(
            src_ref=beyond,
            dst_ref=beyond_in.at[me],
            send_sem=beyond_send,
            recv_sem=beyond_recv,
            device_id=device,
            device_id_type=MESH,
        )

    def over_tile(rel, action):
        def body(d, carry):
            peer = lax.rem(me + d, group)
            action({"member": peer} if rel == 1 else {"member": peer, "gx": (right, 0, left)[rel]})
            return carry

        lax.fori_loop(1 if rel == 1 else 0, group, body, 0)

    inner_rows(0)

    @pl.when(jnp.logical_not(later))
    def _():
        inner_rows(1)
        start_fore(range(EARLY), ())
        pl.semaphore_wait(partner_ready, 1)
        to_across()

    none = jnp.zeros((16, 128), F32)

    @pl.when(core == 0)
    def _():
        edge_rows(0, 1)
        first, second = state[2, 0], state[3, 0]
        outer, inner = advance(none, none, first), advance(none, first, second)
        low_fields[0] = advance(outer, inner, mid[2, 0])
        low_fields[1] = advance(inner, mid[2, 0], mid[3, 0])
        edge[0] = advance(none, none, outer)
        edge[1] = advance(none, outer, inner)

    @pl.when(core == 1)
    def _():
        edge_rows(0, 0)
        first, second = state[17, 0], state[16, 0]
        outer, inner = advance(first, none, none), advance(second, first, none)
        low_fields[15] = advance(mid[15, 0], inner, outer)
        low_fields[14] = advance(mid[14, 0], mid[15, 0], inner)
        edge[0] = advance(inner, outer, none)
        edge[1] = advance(outer, none, none)

    @pl.when(later)
    def _():
        partial[...] = own_samples()

        @pl.when(core == 0)
        def _():
            over_tile(2, lambda device: send_picked(partial, 2, device).start())

        @pl.when(core == 1)
        def _():
            over_tile(0, lambda device: send_picked(partial, 0, device).start())

    @pl.when(later)
    def _():
        inner_rows(1)
        pl.semaphore_wait(group_in, 1)
        signal(mate_in, {"gx": mate})
        start_fore(range(LATER_EARLY), ())
        pl.semaphore_wait(mate_in, 1)

    @pl.when(jnp.logical_not(later))
    def _():
        pl.semaphore_wait(ready, group - 1)
        signal(group_in, {"gx": across})

    @pl.when(core == 0)
    def _():
        edge_rows(0, 0)

    @pl.when(core == 1)
    def _():
        edge_rows(0, 1)

    for direction in range(2):
        to_side(direction).wait_recv()
    picked[...] = own_samples()
    over_tile(1, lambda device: send_picked(picked, 1, device).start())

    @pl.when(core == 0)
    def _():
        over_tile(0, lambda device: send_picked(picked, 0, device).start())

    @pl.when(core == 1)
    def _():
        over_tile(2, lambda device: send_picked(picked, 2, device).start())

    @pl.when(jnp.logical_not(later))
    def _():
        across_col = tile_row(col, across)
        across_x = across_col // 128 - across * 16 - jnp.where(core == 0, 14, 0)
        levels = jnp.where(core == 0, side_in[0, 1:2, :64], side_in[1, 1:2, :64])
        beyond[...] = sample(
            [edge[0], edge[1]],
            hot(across_col),
            (across_x, range(2)),
            levels.astype(jnp.int32),
        )
        beyond_in[me] = beyond[...]
        over_tile(1, lambda device: send_beyond(device).start())

        @pl.when(core == 0)
        def _():
            over_tile(2, lambda device: send_picked(picked, 2, device).start())

        @pl.when(core == 1)
        def _():
            over_tile(0, lambda device: send_picked(picked, 0, device).start())

    @pl.when(later)
    def _():
        beyond_in[...] = jnp.zeros((16, 2, 128), F32)

    picked_in[1, me] = picked[...]

    @pl.when(later)
    def _():
        start_fore(range(LATER_EARLY, 2), ())

    if EARLY < 2:

        @pl.when(jnp.logical_not(later))
        def _():
            start_fore(range(EARLY, 2), ())

    for direction in range(2):
        edge_rows(1, direction)
    start_fore((), range(2))

    @pl.when(later)
    def _():
        start_fore(range(2, 4), range(2, 4))

    @pl.when(jnp.logical_not(later))
    def _():
        start_fore(range(max(EARLY, 2), 4), range(2, 4))

    gathered[:, pl.ds(pl.multiple_of(me * 16, 16), 16), :] = fore[me]

    def three(a, b, c, fill):
        return jnp.concatenate([a, b, c, jnp.full((1, 64), fill, a.dtype)], axis=1)

    before = jnp.maximum(tile - 1, 0)
    after = jnp.minimum(tile + 1, tiles - 1)
    near_col = three(tile_row(col, before), own_col, tile_row(col, after), 0)
    near_radius = three(
        tile_row(radius, before), tile_row(radius, tile), tile_row(radius, after), 1
    ).astype(F32)
    from_left, own, from_right = side_in[0, 0:1, :], side[0:1, :], side_in[1, 0:1, :]
    near_value = three(from_left[:, :64], own[:, :64], from_right[:, :64], 0.0)
    near_var = three(from_left[:, 64:], own[:, 64:], from_right[:, 64:], 1.0)
    lane = lax.broadcasted_iota(jnp.int32, (1, 256), 1)
    first = jnp.where(tile == 0, 64, 0)
    last = jnp.where(tile == tiles - 1, 128, 192)
    valid = (lane >= first) & (lane < last)
    inverse = jnp.where(valid, 1.0 / near_var, 0.0)
    gap_along = (tile * 16 + me - near_col // 128).astype(F32)
    site = 4 * lax.broadcasted_iota(jnp.int32, (32, 256), 0)
    gap_across = (site - lax.rem(near_col, 128)).astype(F32)
    taper = jnp.maximum(
        0.0,
        1.0 - (gap_along * gap_along + gap_across * gap_across) / (near_radius * near_radius),
    )
    wgt[...] = taper * inverse

    def arrived(buffer, count, sem):
        rows = buffer.at[pl.ds(0, count)]
        pltpu.make_async_copy(rows, rows, sem).wait()

    def by_member(buffer):
        rows = jnp.concatenate([buffer[m] for m in range(16)], axis=0)
        return jnp.concatenate([rows[:, :64], rows[:, 64:]], axis=0)

    for rel in range(3):
        arrived(picked_in.at[rel], 15 if rel == 1 else 16, pick_recv.at[rel])

    @pl.when(jnp.logical_not(later))
    def _():
        arrived(beyond_in, 15, beyond_recv)

    added = by_member(beyond_in)
    ensemble = jnp.concatenate(
        [
            by_member(picked_in.at[0]) + jnp.where(core == 0, added, 0.0),
            by_member(picked_in.at[1]),
            by_member(picked_in.at[2]) + jnp.where(core == 1, added, 0.0),
            jnp.zeros((64, 64), F32),
        ],
        axis=1,
    )
    mean = jnp.sum(ensemble, axis=0, keepdims=True) / 64.0
    spread = ensemble - mean
    innovation = near_value - mean
    spread_ref[...] = spread
    spread_hi, spread_lo = split2(spread)
    across_obs = jnp.concatenate([spread_hi, spread_hi, spread_lo, spread_lo], axis=0)

    lane2 = lax.broadcasted_iota(jnp.int32, (64, 128), 1)
    row2 = lax.broadcasted_iota(jnp.int32, (64, 128), 0)
    is_first = lane2 < 64
    eye = (lax.rem(lane2, 64) == row2).astype(F32)
    is_first_row = lax.broadcasted_iota(jnp.int32, (1, 128), 1) < 64

    def operand(x):
        hi, lo = split2(x)
        return jnp.concatenate([hi, lo], axis=1)

    def stationary(x):
        hi = x.astype(BF16).astype(F32)
        lo = x - hi
        zero = jnp.zeros_like(x)
        top = jnp.concatenate(
            [jnp.where(is_first, hi, zero), jnp.where(is_first, lo, zero)], axis=1
        ).astype(BF16)
        bottom = jnp.concatenate(
            [jnp.where(is_first, zero, hi), jnp.where(is_first, zero, lo)], axis=1
        ).astype(BF16)
        return jnp.concatenate([top, bottom, top, bottom], axis=0)

    def fold(x):
        return x[:, :128] + x[:, 128:]

    def solve(batch):
        pairs = [batch * NS_PAIRS + i for i in range(NS_PAIRS)]
        system, drive = [], []
        for p in pairs:
            scaled = [spread_ref[...] * wgt[pl.ds(2 * p + h, 1), :] for h in range(2)]
            both = jnp.concatenate(scaled, axis=0)
            hi, lo = split2(both)
            product = fold(matmul_t(hi, across_obs)) + matmul_t(lo, across_obs[:128])
            system.append(jnp.where(is_first, product[:64], product[64:]) + 63.0 * eye)
            sums = [jnp.sum(s * innovation, axis=1, keepdims=True) for s in scaled]
            drive.append(jnp.where(is_first, sums[0], sums[1]))
        inv_norm, power, root = [], [], []
        for s in system:
            squares = jnp.sum(s * s, axis=0, keepdims=True)
            one = jnp.sum(jnp.where(is_first_row, squares, 0.0), axis=1, keepdims=True)
            two = jnp.sum(jnp.where(is_first_row, 0.0, squares), axis=1, keepdims=True)
            inv = 1.0 / jnp.sqrt(jnp.where(is_first_row, one, two))
            inv_norm.append(inv)
            power.append(s * inv)
        root = [1.5 * eye - 0.5 * p for p in power]
        for sweep in range(NS_ITERS - 1):
            fixed = [stationary(p) for p in power]
            moving = [operand(p) for p in power]
            if sweep == 0:
                square = [fold(matmul(m, f)) for m, f in zip(moving, fixed)]
            else:
                stacked = [
                    fold(matmul(jnp.concatenate([m, operand(z)], axis=0), f))
                    for m, z, f in zip(moving, root, fixed)
                ]
                square = [s[:64] for s in stacked]
                root = [1.5 * z - 0.5 * s[64:] for z, s in zip(root, stacked)]
            cube = [fold(matmul(operand(s), f)) for s, f in zip(square, fixed)]
            power = [2.25 * p - 1.5 * s + 0.25 * c for p, s, c in zip(power, square, cube)]
        root = [
            1.5 * z - 0.5 * fold(matmul(operand(z), stationary(p))) for z, p in zip(root, power)
        ]
        for p, z, inv, d in zip(pairs, root, inv_norm, drive):
            through = jnp.sum(z * d, axis=0, keepdims=True)
            again = z * through
            one = jnp.sum(jnp.where(is_first, again, 0.0), axis=1, keepdims=True)
            two = jnp.sum(jnp.where(is_first, 0.0, again), axis=1, keepdims=True)
            w = jnp.sqrt(63.0 * inv) * z + jnp.where(is_first, one, two) * inv
            w = w + (1.0 - jnp.sum(w, axis=0, keepdims=True)) * (1.0 / 64.0)
            hi = w.astype(BF16).astype(F32)
            lo = w - hi
            weights[2 * p] = jnp.where(is_first, hi, pltpu.roll(lo, 64, 1)).astype(BF16)
            weights[2 * p + 1] = jnp.where(is_first, pltpu.roll(hi, 64, 1), lo).astype(BF16)

    y8 = lax.broadcasted_iota(jnp.int32, (1, 8, 128), 1).astype(F32) * 0.25
    half = lax.broadcasted_iota(jnp.int32, (1, 8, 128), 2) < 64
    tent = [jnp.maximum(0.0, 1.0 - jnp.abs(y8 - c)) for c in range(3)]
    coef_a = jnp.where(half, tent[0], tent[1])
    coef_b = jnp.where(half, tent[2], 0.0)

    def all_bytes(buffer, sem):
        rows = buffer.at[pl.ds(0, buffer.shape[0] // group * (group - 1))]
        return pltpu.make_async_copy(rows, rows, sem)

    def send_back(half, peer):
        return pltpu.make_async_remote_copy(
            src_ref=back.at[half, pl.ds(pl.multiple_of(peer * 32, 32), 32), :],
            dst_ref=back_in.at[half, pl.ds(pl.multiple_of(me * 32, 32), 32), :],
            send_sem=back_send.at[half],
            recv_sem=back_recv.at[half],
            device_id={"member": peer},
            device_id_type=MESH,
        )

    def keep(half):
        rows = pl.ds(pl.multiple_of(me * 32, 32), 32)
        return pltpu.make_async_copy(
            back.at[half, rows], back_in.at[half, rows], keep_sem.at[half]
        )

    def turn(half, fh):
        piece = 2 * (1 - half) + fh
        all_bytes(gathered.at[piece], fore_recv.at[piece]).wait()
        for fl in range(4):
            rows = jnp.concatenate(
                [gathered[piece, pl.ds(fl + 4 * odd, 32, stride=8), :] for odd in range(2)], axis=0
            )
            columns = jnp.concatenate([rows, rows], axis=0).T
            turned[4 * fh + fl] = columns[:64]
            turned[8 + 4 * fh + fl] = columns[64:]

    def blend(half, part):
        block = half * 8 + part
        rows = turned[:, 8 * part : 8 * part + 8, :]
        near = operand((rows * coef_a).reshape(128, 128))
        far = operand((rows * coef_b).reshape(128, 128))
        c01 = weights[pl.ds(2 * block, 2)].reshape(128, 128)
        c23 = weights[pl.ds(2 * block + 2, 2)].reshape(128, 128)
        product = matmul(near, jnp.concatenate([c01, c01], axis=0)) + matmul(
            far, jnp.concatenate([c23, c23], axis=0)
        )
        product = (product[:, :64] + product[:, 64:]).reshape(8, 2, 8, 64)
        for odd in range(2):
            stage[:, 64 * odd + 8 * part : 64 * odd + 8 * part + 8, :] = product[:, odd]

    def half_step(step, carry):
        half = 1 - step
        for fh in range(2):
            turn(half, fh)
        solve(half)

        @pl.when(step == 0)
        def _():
            weights[32] = weights[31]
            weights[33] = jnp.zeros((64, 128), BF16)

        for part in range(8):
            blend(half, part)
        for pair in range(8):
            rows = stage[pair].T
            for odd in range(2):
                back[half, pl.ds(pair + 8 * odd, 32, stride=16), :] = rows[
                    32 * odd : 32 * odd + 32
                ]
        over_peers(lambda peer: send_back(half, peer).start())
        keep(half).start()
        return carry

    lax.fori_loop(0, 2, half_step, 0)

    for part in range(2):
        for direction in range(2):
            halo(direction, part).wait_send()
    for direction in range(2):
        to_side(direction).wait_send()
    for rel in range(3):
        arrived(picked_in.at[rel], 15 if rel == 1 else 16, pick_send.at[rel])

    @pl.when(jnp.logical_not(later))
    def _():
        arrived(beyond_in, 15, beyond_send)

    for fh in range(4):
        all_bytes(gathered.at[fh], fore_send.at[fh]).wait()
    for half in range(2):
        all_bytes(back.at[half], back_send.at[half]).wait()
        keep(half).wait()
    for half in range(2):
        all_bytes(back.at[half], back_recv.at[half]).wait()


def place(back_in, out, landed, placed, load_sem, leave_sem):
    lane = lax.broadcasted_iota(jnp.int32, (16, 128), 1)
    flat = landed.reshape(4, 2, 128, 128)

    def load(k):
        return pltpu.make_async_copy(back_in.at[:, :, k], landed.at[k], load_sem.at[k])

    def leave(k):
        return pltpu.make_async_copy(placed.at[k], out.at[k], leave_sem.at[k])

    for k in range(4):
        load(k).start()
    for k in range(4):
        load(k).wait()
        for pair in range(8):
            low, high = [flat[k, half, pl.ds(pair, 16, stride=8), :] for half in range(2)]
            placed[k, 2 * pair] = jnp.where(lane < 64, low, pltpu.roll(high, 64, 1))
            placed[k, 2 * pair + 1] = jnp.where(lane < 64, pltpu.roll(low, 64, 1), high)
        leave(k).start()
    for k in range(4):
        leave(k).wait()


def per_device(background_fields, obs_col, measured_height, obs_radius, obs_value, obs_var):
    dma = pltpu.SemaphoreType.DMA
    result = pl.pallas_call(
        kernel,
        out_shape=jax.ShapeDtypeStruct((2, 512, 128), F32),
        in_specs=[pl.BlockSpec(memory_space=pltpu.HBM)] * 6,
        out_specs=pl.BlockSpec(memory_space=pltpu.HBM),
        scratch_shapes=[
            pltpu.VMEM((1024, 128), F32),
            pltpu.VMEM((16, 128), jnp.int32),
            pltpu.VMEM((16, 128), jnp.int32),
            pltpu.VMEM((1, 64), jnp.int32),
            pltpu.VMEM((1, 64), F32),
            pltpu.VMEM((1, 64), F32),
            pltpu.VMEM((20, 4, 16, 128), F32),
            pltpu.VMEM((18, 4, 16, 128), F32),
            pltpu.VMEM((16, 16, 128), F32),
            pltpu.VMEM((16, 4, 16, 128), F32),
            pltpu.VMEM((4, 256, 128), F32),
            pltpu.VMEM((16, 64, 128), F32),
            pltpu.VMEM((34, 64, 128), BF16),
            pltpu.VMEM((32, 256), F32),
            pltpu.VMEM((64, 256), F32),
            pltpu.VMEM((8, 128), F32),
            pltpu.VMEM((2, 8, 128), F32),
            pltpu.VMEM((2, 128), F32),
            pltpu.VMEM((2, 128), F32),
            pltpu.VMEM((2, 128), F32),
            pltpu.VMEM((2, 16, 128), F32),
            pltpu.VMEM((3, 16, 2, 128), F32),
            pltpu.VMEM((16, 2, 128), F32),
            pltpu.VMEM((8, 128, 64), F32),
            pltpu.VMEM((2, 512, 128), F32),
            dma((6,)),
            dma((4,)),
            dma((4,)),
            dma((2,)),
            dma((2,)),
            dma((3,)),
            dma((3,)),
            dma,
            dma,
            pltpu.SemaphoreType.REGULAR,
            pltpu.SemaphoreType.REGULAR,
            pltpu.SemaphoreType.REGULAR,
            pltpu.SemaphoreType.REGULAR,
            dma((4,)),
            dma((4,)),
            dma((2,)),
            dma((2,)),
            dma((2,)),
        ],
        compiler_params=pltpu.CompilerParams(
            collective_id=0, has_side_effects=True, vmem_limit_bytes=64 * 1024 * 1024
        ),
    )(
        *(
            pltpu.with_memory_space_constraint(x, pltpu.HBM)
            for x in (
                background_fields.reshape(1024, 128),
                obs_col.reshape(16, 128),
                obs_radius.reshape(16, 128),
                measured_height.reshape(1, 64),
                obs_value.reshape(1, 64),
                obs_var.reshape(1, 64),
            )
        )
    )
    return pl.pallas_call(
        place,
        out_shape=jax.ShapeDtypeStruct((4, 16, 16, 128), F32),
        in_specs=[pl.BlockSpec(memory_space=pltpu.HBM)],
        out_specs=pl.BlockSpec(memory_space=pltpu.HBM),
        scratch_shapes=[
            pltpu.VMEM((4, 2, 16, 8, 128), F32),
            pltpu.VMEM((4, 16, 16, 128), F32),
            dma((4,)),
            dma((4,)),
        ],
        compiler_params=pltpu.CompilerParams(vmem_limit_bytes=60 * 1024 * 1024),
    )(result.reshape(2, 16, 4, 8, 128))


def solution(mesh):
    return jax.shard_map(
        per_device,
        mesh=mesh,
        in_specs=(P("member", None, "gx", None), P(), P("gx"), P(), P("gx"), P("gx")),
        out_specs=P("member", None, "gx", None),
        check_vma=False,
    )
```
